32 devices in a mesh: sec: 2 (over y), circ: 4 (over x, core), rad: 4 (over z).
Axes of the slice: x: 2, y: 2, z: 4, core: 2. Of those that a mesh axis runs over, the one named last changes fastest.
Arguments:
- adjoint: float32 [2, 5, 8, 64, 512], P('sec', None, None, 'rad', 'circ'), may hold values from -6 to 6
- source: float32 [2, 5, 8, 64, 512], P('sec', None, None, 'rad', 'circ'), may hold values from -6 to 6
- jacobian: float32 [2, 5, 5, 8, 64, 512], P('sec', None, None, None, 'rad', 'circ'), may hold values from -2 to 2
- couple: float32 [2, 12, 8, 64, 512], P('sec', None, None, 'rad', 'circ'), may hold values from 0.05 to 1
- donor_row: int32 [4, 4, 4, 6], P('rad'), may hold values from 0 to 15, as said below
- target_row: int32 [4, 4, 4, 6], P('rad'), may hold values from 0 to 15, as said below
- tile_count: int32 [4, 4, 4], P('rad'), may hold values from 0 to 6, as said below
- weights: float32 [4, 4, 4, 6, 128], P('rad', None, 'circ'), may hold values from 0.2 to 1
Outputs:
- swept: float32 [2, 5, 8, 64, 512], P('sec', None, None, 'rad', 'circ')
The draws below stay inside these ranges and needn't reach their ends.
Inputs may be any that keep to these rules, and one draw needn't show every extreme that they name: `tile_count`: counts are ragged over all pairs of a radial index; in every draw some stator device receives 6 tiles from every rotor device of its radial index. `donor_row`: entries at slots at or past the pair's tile_count are not read. `target_row`: each target row lies within one row of its donor row. Entries at slots at or past the pair's tile_count are not read.
All inputs are finite; a program needn't handle non-finite values.
Results may differ from the reference program's by a relative error of at most 0.000075.
Values sent between devices are 32-bit elements; how exact they have to be, the bound alone decides.
No kernel may reach another device: no remote copies, remote signals or barrier semaphores. Data moves between devices by JAX's collectives and lax.ppermute only.
A program may use at most 64 MiB of HBM per device.

```python
import math
import jax
import jax.numpy as jnp

VARS = 5
NA = 8
CR = 16
CC = 128
MAXT = 6
SWEEPS = 3
NR = 64
NC = 512
N_CIRC = 4
N_RAD = 4


def rows_pair(key):
    inner = jax.random.fold_in(key, 11)
    first, second = jax.random.split(inner)
    donor = jax.random.randint(first, (N_RAD, N_CIRC, N_CIRC, MAXT), 0, CR)
    delta = jax.random.randint(second, (N_RAD, N_CIRC, N_CIRC, MAXT), -1, 2)
    target = jnp.clip(donor + delta, 0, CR - 1)
    return (donor.astype(jnp.int32), target.astype(jnp.int32))


def draw_donor_row(key, part):
    return rows_pair(key)[0]


def draw_target_row(key, part):
    return rows_pair(key)[1]


def draw_tile_count(key, part):
    inner = jax.random.fold_in(key, 23)
    first, second, third = jax.random.split(inner, 3)
    counts = jax.random.randint(first, (N_RAD, N_CIRC, N_CIRC), 0, MAXT + 1)
    rad_pick = jax.random.randint(second, (), 0, N_RAD)
    reader_pick = jax.random.randint(third, (), 0, N_CIRC)
    rad_ids = jnp.arange(N_RAD)[:, None, None]
    reader_ids = jnp.arange(N_CIRC)[None, None, :]
    full = (rad_ids == rad_pick) & (reader_ids == reader_pick)
    return jnp.where(full, MAXT, counts).astype(jnp.int32)


def level_of(rng, shape, shards, least, largest):
    gain = 1.0
    for axis_at, parts in shards:
        draws = jax.random.uniform(jax.random.fold_in(jax.random.fold_in(rng, 6), axis_at), (parts,), jnp.float32, least / len(shards), largest / len(shards))
        gain = gain * jnp.repeat(jnp.exp(draws), shape[axis_at] // parts).reshape((-1,) + (1,) * (len(shape) - 1 - axis_at))
    return gain


def scatter_about(own_key, dims, deviation, reach, cuts=(), held_as=jnp.bfloat16):
    values = deviation * jax.random.normal(own_key, dims, jnp.float32)
    if cuts:
        values = values * level_of(own_key, dims, cuts, -0.22, 0.18)
    return jnp.clip(values, -reach, reach).astype(held_as)


def setup_inputs(seed: int = 0) -> dict:
    key_list = jax.random.split(jax.random.key(seed), 9)
    adjoint = scatter_about(key_list[0], (2, VARS, NA, NR, NC), 1.0, 6.0, ((0, 2), (3, 4), (4, 4)), jnp.float32)
    source = scatter_about(key_list[1], (2, VARS, NA, NR, NC), 1.0, 6.0, ((0, 2), (3, 4), (4, 4)), jnp.float32)
    jacobian = scatter_about(key_list[2], (2, VARS, VARS, NA, NR, NC), 10 ** -0.5, 2.0, ((0, 2), (4, 4), (5, 4)), jnp.float32)
    couple = jnp.clip(jnp.exp(math.log(1.0) - 2.9957323 * jax.random.uniform(key_list[3], (2, 12, NA, NR, NC), jnp.float32) ** level_of(key_list[3], (2, 12, NA, NR, NC), ((0, 2), (3, 4), (4, 4)), -0.2, 0.2)), 0.05, 1.0)
    donor_row = draw_donor_row(jax.random.fold_in(key_list[8], 71), 0)
    target_row = draw_target_row(jax.random.fold_in(key_list[8], 71), 0)
    tile_count = draw_tile_count(jax.random.fold_in(key_list[8], 71), 0)
    weights = jnp.clip(0.2 + 0.8 * jax.random.uniform(key_list[7], (N_RAD, N_CIRC, N_CIRC, MAXT, CC), jnp.float32) ** level_of(key_list[7], (N_RAD, N_CIRC, N_CIRC, MAXT, CC), ((0, 4), (2, 4)), -0.2, 0.2), 0.2, 1.0)
    return dict(adjoint=adjoint, source=source, jacobian=jacobian, couple=couple, donor_row=donor_row, target_row=target_row, tile_count=tile_count, weights=weights)


def neighbours(field):
    axial = jnp.pad(field, ((0, 0), (0, 0), (2, 2), (0, 0), (0, 0)))
    radial = jnp.pad(field, ((0, 0), (0, 0), (0, 0), (2, 2), (0, 0)))
    na = field.shape[2]
    nr = field.shape[3]
    result = []
    for off in (-2, -1, 1, 2):
        result.append(axial[:, :, 2 + off:2 + off + na])
    for off in (-2, -1, 1, 2):
        result.append(radial[:, :, :, 2 + off:2 + off + nr])
    for off in (-2, -1, 1, 2):
        result.append(jnp.roll(field, -off, axis=4))
    return result


def reference(adjoint, source, jacobian, couple, donor_row, target_row, tile_count, weights):
    face = adjoint[0, :, NA - 2:, :, :]
    face = face.reshape(VARS, 2, N_RAD, CR, N_CIRC, CC).transpose(2, 3, 4, 0, 1, 5)
    rad_ids = jnp.arange(N_RAD, dtype=jnp.int32)[:, None, None, None]
    donor_ids = jnp.arange(N_CIRC, dtype=jnp.int32)[None, :, None, None]
    reader_ids = jnp.arange(N_CIRC, dtype=jnp.int32)[None, None, :, None]
    tiles = face[rad_ids, donor_row, donor_ids]
    live = (jnp.arange(MAXT, dtype=jnp.int32)[None, None, None, :] < tile_count[..., None]).astype(jnp.float32)
    scale = weights * live[..., None]
    contrib = tiles * scale[:, :, :, :, None, None, :]
    inflow = jnp.zeros((N_RAD, CR, N_CIRC, VARS, 2, CC), jnp.float32)
    inflow = inflow.at[rad_ids, target_row, reader_ids].add(contrib)
    inflow = inflow.transpose(3, 4, 0, 1, 2, 5).reshape(VARS, 2, NR, NC)
    stator_rhs = source[1].at[:, 0:2].add(inflow)
    rhs = jnp.stack([source[0], stator_rhs])
    pivot = 1.0 + jnp.sum(couple, axis=1)
    lam = adjoint
    for sweep in range(SWEEPS):
        near = neighbours(lam)
        total = jnp.zeros_like(lam)
        for index in range(12):
            total = total + couple[:, index][:, None] * near[index]
        turned = jnp.zeros_like(lam)
        for column in range(VARS):
            turned = turned + jacobian[:, :, column] * total[:, column][:, None]
        lam = (rhs + turned) / pivot[:, None]
    return lam
```

```python
import jax
import jax.numpy as jnp
from jax import lax
from jax.experimental import pallas as pl
from jax.experimental.pallas import tpu as pltpu
from jax.sharding import PartitionSpec as P

SWEEPS = 3
AXES = ("sec", "circ", "rad")
SUB, LANES = 8, 128
GROUP = 20
PARAMS = pltpu.CompilerParams(vmem_limit_bytes=16 * 1024 * 1024)


def routes(mesh):
    secs, circs, rads = (mesh.shape[a] for a in AXES)

    def pairs(target):
        flat = lambda s, c, r: (s * circs + c) * rads + r
        return [
            (flat(s, c, r), flat(*target(s, c, r)))
            for s in range(secs)
            for c in range(circs)
            for r in range(rads)
        ]

    def snake(s, c, r):
        if c % 2 == 0:
            return (s, c, r + 1) if r < rads - 1 else (s, c + 1, r)
        return (s, c, r - 1) if r > 0 else (s, c - 1, r)

    ahead = pairs(snake)
    return {
        "ahead": ahead,
        "back": [(b, a) for a, b in ahead],
        "mate": pairs(lambda s, c, r: (s, c ^ 1, r)),
        "across": pairs(lambda s, c, r: (s, (c - 1 if c % 2 == 0 else c + 1) % circs, r)),
        "faces": [
            pairs(lambda s, c, r: (1, (c + k) % circs, r) if s == 0 else (0, (c - k) % circs, r))
            for k in range(0, circs, 2)
        ],
    }


def iotas():
    sub = lax.broadcasted_iota(jnp.int32, (SUB, LANES), 0)
    lane = lax.broadcasted_iota(jnp.int32, (SUB, LANES), 1)
    return sub, lane


def down(x, by):
    return pltpu.roll(x, by % SUB, 0) if by % SUB else x


def along(x, by):
    return pltpu.roll(x, by % LANES, 1) if by % LANES else x


class Packer:
    def __init__(self, na, nv):
        self.sub, self.lane = iotas()
        self.na = na
        self.low, self.high, self.cols = {}, {}, {}

    def put(self, book, key, keep, x):
        book[key] = jnp.where(keep, x, book[key]) if key in book else x

    def add(self, v, a, half, x):
        k = v * self.na + a
        group, j = k // 4, k % 4
        inside = (self.sub >= 2 * j) & (self.sub < 2 * j + 2)
        if half == 0:
            self.put(self.low, group, inside, down(x, 2 * j))
        else:
            self.put(self.high, group, inside, down(x, 2 * j + 2))
        spot = 4 * (k % GROUP)
        inside = (self.lane >= spot) & (self.lane < spot + 4)
        self.put(self.cols, (k // GROUP, half), inside, along(x, spot + 2))

    def write(self, ahead_ref, back_ref, cols_ref):
        even = lax.axis_index("circ") % 2 == 0
        for g in range(len(self.low)):
            rows = slice(SUB * g, SUB * (g + 1))
            ahead_ref[rows, :] = jnp.where(even, self.high[g], self.low[g])
            back_ref[rows, :] = jnp.where(even, self.low[g], self.high[g])
        for (part, half), x in self.cols.items():
            at = SUB * (2 * part + half)
            cols_ref[at : at + SUB, :] = x


def pack_kernel(lam_ref, ahead_ref, back_ref, cols_ref, face_ref):
    nv, na = lam_ref.shape[:2]
    packer = Packer(na, nv)
    for v in range(nv):
        for a in range(na):
            for half in range(2):
                rows = slice(SUB * half, SUB * (half + 1))
                x = lam_ref[v, a, rows, :]
                packer.add(v, a, half, x)
                if a >= na - 2:
                    face_ref[v, a - (na - 2), rows, :] = x
    packer.write(ahead_ref, back_ref, cols_ref)


def taps_kernel(donors_ref, targets_ref, counts_ref, weights_ref, after_ref, taps_ref):
    me = lax.axis_index("circ")
    stator = lax.axis_index("sec") == 1
    sub, _ = iotas()
    slots = donors_ref.shape[-1]
    for d in range(donors_ref.shape[0]):
        acc = {(t, h): jnp.zeros((SUB, LANES), jnp.float32) for t in range(3) for h in range(2)}
        for k in range(slots):
            live = (k < counts_ref[d, me]) & stator
            target = targets_ref[d, me, k]
            step = target - donors_ref[d, me, k]
            w = jnp.broadcast_to(weights_ref[d * slots + k : d * slots + k + 1, :], (SUB, LANES))
            for t in range(3):
                row = jnp.where(live & (step == t - 1), target, -1)
                for h in range(2):
                    acc[t, h] += jnp.where(sub + SUB * h == row, w, 0.0)
        for (t, h), x in acc.items():
            taps_ref[d, t, SUB * h : SUB * (h + 1), :] = x


def local_kernel(first, *refs):
    lam_ref, couple_ref, _, near_ref = refs[:4]
    nv, na = lam_ref.shape[:2]
    sub, lane = iotas()
    for a in range(na):
        coef = []
        for half in range(2):
            rows = slice(SUB * half, SUB * (half + 1))
            c = [couple_ref[i, a, rows, :] for i in range(12)]
            if first:
                total = c[0]
                for i in range(1, 12):
                    total = total + c[i]
                refs[4][a, rows, :] = 1.0 / (1.0 + total)
            if half == 0:
                c[4] = jnp.where(sub >= 2, c[4], 0.0)
                c[5] = jnp.where(sub >= 1, c[5], 0.0)
            else:
                c[6] = jnp.where(sub < SUB - 1, c[6], 0.0)
                c[7] = jnp.where(sub < SUB - 2, c[7], 0.0)
            c[8] = jnp.where(lane >= 2, c[8], 0.0)
            c[9] = jnp.where(lane >= 1, c[9], 0.0)
            c[10] = jnp.where(lane < LANES - 1, c[10], 0.0)
            c[11] = jnp.where(lane < LANES - 2, c[11], 0.0)
            coef.append(c)
        for v in range(nv):
            x = [lam_ref[v, a, SUB * h : SUB * (h + 1), :] for h in range(2)]
            moved = {o: [down(x[h], -o) for h in range(2)] for o in (-2, -1, 1, 2)}
            for half in range(2):
                rows = slice(SUB * half, SUB * (half + 1))
                c = coef[half]
                total = None
                for i, o in enumerate((-2, -1, 1, 2)):
                    if 0 <= a + o < na:
                        term = c[i] * lam_ref[v, a + o, rows, :]
                        total = term if total is None else total + term
                for i, o in enumerate((-2, -1, 1, 2)):
                    m = moved[o]
                    if o < 0:
                        y = m[0] if half == 0 else jnp.where(sub >= -o, m[1], m[0])
                    else:
                        y = m[1] if half == 1 else jnp.where(sub < SUB - o, m[0], m[1])
                    total = total + c[4 + i] * y
                for i, o in enumerate((-2, -1, 1, 2)):
                    total = total + c[8 + i] * along(x[half], -o)
                near_ref[v, a, rows, :] = total


def finish_kernel(faces, last, *refs):
    near_ref, couple_ref, jac_ref, src_ref, inv_ref, ahead_ref, back_ref, mate_ref, across_ref = refs[:9]
    face_refs = refs[9 : 9 + faces]
    rest = refs[9 + faces :]
    if faces:
        taps_ref, out_ref, rhs_ref = rest[0], rest[1], rest[2]
        rest = rest[3:]
    else:
        out_ref, rhs_ref = rest[0], src_ref
        rest = rest[1:]
    nv, na = near_ref.shape[:2]
    sub, lane = iotas()
    circs, rads = lax.axis_size("circ"), lax.axis_size("rad")
    me, rad = lax.axis_index("circ"), lax.axis_index("rad")
    even = me % 2 == 0
    has_low = rad > 0
    has_high = rad < rads - 1

    low_rows, high_rows = [], []
    for g in range(nv * na // 4):
        rows = slice(SUB * g, SUB * (g + 1))
        x, y = ahead_ref[rows, :], back_ref[rows, :]
        low_rows.append(jnp.where(even, x, y))
        high_rows.append(jnp.where(even, y, x))

    wide, slim = {}, {}
    for part in range(nv * na // GROUP):
        for half in range(2):
            at = SUB * (2 * part + half)
            x, y = mate_ref[at : at + SUB, :], across_ref[at : at + SUB, :]
            right = along(jnp.where(even, x, y), -2)
            left = along(jnp.where(even, y, x), 2)
            wide[part, half] = jnp.where(lane % 4 < 2, right, left)
            slim[part, half] = jnp.where(lane % 4 < 2, along(right, 1), along(left, -1))

    packer = None if last else Packer(na, nv)
    for a in range(na):
        for half in range(2):
            rows = slice(SUB * half, SUB * (half + 1))
            c = [couple_ref[i, a, rows, :] for i in range(4, 12)]
            if half == 0:
                far = jnp.where((sub < 2) & has_low, c[0], 0.0)
                nigh = jnp.where((sub < 1) & has_low, c[1], 0.0)
            else:
                far = jnp.where((sub >= SUB - 2) & has_high, c[3], 0.0)
                nigh = jnp.where((sub >= SUB - 1) & has_high, c[2], 0.0)
            outer = jnp.where(lane < 2, c[4], jnp.where(lane >= LANES - 2, c[7], 0.0))
            inner = jnp.where(lane < 1, c[5], jnp.where(lane >= LANES - 1, c[6], 0.0))
            near = []
            for v in range(nv):
                k = v * na + a
                j = k % 4
                if half == 0:
                    m = low_rows[k // 4]
                    y2, y1 = down(m, -2 * j), down(m, -2 * j - 1)
                else:
                    m = high_rows[k // 4]
                    y2, y1 = down(m, 6 - 2 * j), down(m, 7 - 2 * j)
                spot = 4 * (k % GROUP)
                key = (k // GROUP, half)
                total = near_ref[v, a, rows, :] + (far * y2 + nigh * y1)
                total = total + outer * along(wide[key], LANES - 2 - spot)
                total = total + inner * along(slim[key], LANES - 2 - spot)
                near.append(total)
            inv = inv_ref[a, rows, :]
            for s in range(nv):
                acc = src_ref[s, a, rows, :]
                if faces and a < 2:
                    for n, face_ref in enumerate(face_refs):
                        donor = (me if n % 2 == 0 else me + 1 - 2 * (me % 2)) - (n // 2) * 2
                        donor = lax.rem(donor + circs, circs)
                        f = [face_ref[s, a, SUB * h : SUB * (h + 1), :] for h in range(2)]
                        before = down(f[half], 1)
                        after = down(f[half], -1)
                        if half == 1:
                            before = jnp.where(sub >= 1, before, down(f[0], 1))
                        else:
                            after = jnp.where(sub < SUB - 1, after, down(f[1], -1))
                        acc = acc + taps_ref[donor, 0, rows, :] * after
                        acc = acc + taps_ref[donor, 1, rows, :] * f[half]
                        acc = acc + taps_ref[donor, 2, rows, :] * before
                if faces:
                    rhs_ref[s, a, rows, :] = acc
                for b in range(nv):
                    acc = acc + jac_ref[s, b, a, rows, :] * near[b]
                x = acc * inv
                out_ref[s, a, rows, :] = x
                if packer is not None:
                    packer.add(s, a, half, x)
    if packer is not None:
        packer.write(*rest)


def whole(count):
    return [pl.BlockSpec(memory_space=pltpu.VMEM)] * count


def call(kernel, outs, args, specs, name):
    specs = [pl.BlockSpec(memory_space=pltpu.VMEM)] * len(args) if specs is None else specs
    return pl.pallas_call(
        kernel,
        out_shape=outs,
        in_specs=specs,
        out_specs=whole(len(outs)),
        compiler_params=PARAMS,
        name=name,
    )(*args)


def solution(mesh):
    route = routes(mesh)
    vmem = lambda *shape: pltpu.VMEM(shape, jnp.float32)

    def sent(x, pairs):
        return lax.ppermute(x, AXES, pairs)

    def per_device(adjoint, source, jacobian, couple, donor_row, target_row, tile_count, weights):
        lam, src, jac, cpl = adjoint[0], source[0], jacobian[0], couple[0]
        nv, na, nr, nc = lam.shape
        slots = donor_row.shape[-1]
        edges = [vmem(2 * nv * na, nc), vmem(2 * nv * na, nc), vmem(4 * SUB, nc)]
        anyspec = pl.BlockSpec(memory_space=pl.ANY)
        vspec = pl.BlockSpec(memory_space=pltpu.VMEM)
        sspec = pl.BlockSpec(memory_space=pltpu.SMEM)

        *msgs, face = call(pack_kernel, edges + [vmem(nv, 2, nr, nc)], [lam], None, "pack")
        rhs, inv, faces, taps = src, None, [], None
        for sweep in range(SWEEPS):
            if sweep == 0:
                direct = [sent(face, pairs) for pairs in route["faces"]]
            ahead = sent(msgs[0], route["ahead"])
            back = sent(msgs[1], route["back"])
            across = sent(msgs[2], route["across"])
            mate = sent(msgs[2], route["mate"])
            first, last = sweep == 0, sweep == SWEEPS - 1
            outs = [vmem(nv, na, nr, nc)] + ([vmem(na, nr, nc)] if first else [])
            near, *more = call(
                lambda *refs, first=first: local_kernel(first, *refs),
                outs, [lam, cpl, mate], [vspec, vspec, anyspec], f"local{sweep}",
            )
            if first:
                inv = more[0]
                for x in direct:
                    faces += [x, sent(x, route["mate"])]
                taps = call(
                    taps_kernel,
                    [vmem(donor_row.shape[1], 3, nr, nc)],
                    [donor_row[0], target_row[0], tile_count[0],
                     weights.reshape(-1, nc), mate],
                    [sspec, sspec, sspec, vspec, anyspec], "taps",
                )[0]
            extra = faces + [taps] if first else []
            if last:
                outs = [jax.ShapeDtypeStruct((nv, na, nr, nc), jnp.float32)]
            else:
                outs = [vmem(nv, na, nr, nc)] + ([vmem(nv, na, nr, nc)] if first else []) + edges
            res = call(
                lambda *refs, n=len(faces) if first else 0, last=last: finish_kernel(n, last, *refs),
                outs, [near, cpl, jac, rhs, inv, ahead, back, mate, across] + extra, None, f"finish{sweep}",
            )
            lam = res[0]
            if first:
                rhs = res[1]
            msgs = res[2:] if first else res[1:]
        return lam[None]

    in_specs = (
        P("sec", None, None, "rad", "circ"),
        P("sec", None, None, "rad", "circ"),
        P("sec", None, None, None, "rad", "circ"),
        P("sec", None, None, "rad", "circ"),
        P("rad", None, None, None),
        P("rad", None, None, None),
        P("rad", None, None),
        P("rad", None, "circ", None, None),
    )
    out_specs = P("sec", None, None, "rad", "circ")
    return jax.shard_map(
        per_device, mesh=mesh, in_specs=in_specs, out_specs=out_specs, check_vma=False
    )
```

```python
import jax
import jax.numpy as jnp
from jax import lax
from jax.experimental import pallas as pl
from jax.experimental.pallas import tpu as pltpu
from jax.sharding import PartitionSpec as P

SWEEPS = 3
AXES = ("sec", "circ", "rad")
SUB, LANES = 8, 128
GROUP = 20
PARAMS = pltpu.CompilerParams(vmem_limit_bytes=16 * 1024 * 1024)


def routes(mesh):
    secs, circs, rads = (mesh.shape[a] for a in AXES)

    def pairs(target):
        flat = lambda s, c, r: (s * circs + c) * rads + r
        return [
            (flat(s, c, r), flat(*target(s, c, r)))
            for s in range(secs)
            for c in range(circs)
            for r in range(rads)
        ]

    def snake(s, c, r):
        if c % 2 == 0:
            return (s, c, r + 1) if r < rads - 1 else (s, c + 1, r)
        return (s, c, r - 1) if r > 0 else (s, c - 1, r)

    ahead = pairs(snake)
    return {
        "ahead": ahead,
        "back": [(b, a) for a, b in ahead],
        "mate": pairs(lambda s, c, r: (s, c ^ 1, r)),
        "across": pairs(lambda s, c, r: (s, (c - 1 if c % 2 == 0 else c + 1) % circs, r)),
        "faces": [
            pairs(lambda s, c, r: (1, (c + k) % circs, r) if s == 0 else (0, (c - k) % circs, r))
            for k in range(0, circs, 2)
        ],
    }


def iotas():
    sub = lax.broadcasted_iota(jnp.int32, (SUB, LANES), 0)
    lane = lax.broadcasted_iota(jnp.int32, (SUB, LANES), 1)
    return sub, lane


def down(x, by):
    return pltpu.roll(x, by % SUB, 0) if by % SUB else x


def along(x, by):
    return pltpu.roll(x, by % LANES, 1) if by % LANES else x


class Packer:
    def __init__(self, na, nv):
        self.sub, self.lane = iotas()
        self.na = na
        self.low, self.high, self.cols = {}, {}, {}

    def put(self, book, key, keep, x):
        book[key] = jnp.where(keep, x, book[key]) if key in book else x

    def add(self, v, a, half, x):
        k = v * self.na + a
        group, j = k // 4, k % 4
        inside = (self.sub >= 2 * j) & (self.sub < 2 * j + 2)
        if half == 0:
            self.put(self.low, group, inside, down(x, 2 * j))
        else:
            self.put(self.high, group, inside, down(x, 2 * j + 2))
        spot = 4 * (k % GROUP)
        inside = (self.lane >= spot) & (self.lane < spot + 4)
        self.put(self.cols, (k // GROUP, half), inside, along(x, spot + 2))

    def write(self, ahead_ref, back_ref, cols_ref):
        even = lax.axis_index("circ") % 2 == 0
        for g in range(len(self.low)):
            rows = slice(SUB * g, SUB * (g + 1))
            ahead_ref[rows, :] = jnp.where(even, self.high[g], self.low[g])
            back_ref[rows, :] = jnp.where(even, self.low[g], self.high[g])
        for (part, half), x in self.cols.items():
            at = SUB * (2 * part + half)
            cols_ref[at : at + SUB, :] = x


def pack_kernel(adjoint_ref, donors_in, ahead_ref, back_ref, cols_ref, *refs):
    *tile_refs, lam_ref, donors_ref, sems = refs
    nv, na, nr, _ = lam_ref.shape
    listed = pltpu.make_async_copy(donors_in, donors_ref, sems.at[nv])
    listed.start()
    copies = [pltpu.make_async_copy(adjoint_ref.at[v], lam_ref.at[v], sems.at[v]) for v in range(nv)]
    for copy in copies:
        copy.start()
    packer = Packer(na, nv)
    for v in range(nv):
        copies[v].wait()
        for a in range(na):
            for half in range(2):
                packer.add(v, a, half, lam_ref[v, a, SUB * half : SUB * (half + 1), :])
    packer.write(ahead_ref, back_ref, cols_ref)
    listed.wait()
    me, circs, slots = lax.axis_index("circ"), donors_ref.shape[1], donors_ref.shape[2]
    for n, tile_ref in enumerate(tile_refs):
        reader = lax.rem(me + 2 * n, circs)
        for part, to in enumerate((reader, reader + 1 - 2 * (reader % 2))):
            for k in range(slots):
                row = jnp.clip(donors_ref[me, to, k], 0, nr - 1)
                for v in range(nv):
                    for a in range(2):
                        at = ((part * slots + k) * nv + v) * 2 + a
                        tile_ref[at : at + 1, :] = lam_ref[v, na - 2 + a, pl.ds(row, 1), :]


def place_weights(targets_ref, counts_ref, weights_ref, placed_ref):
    me = lax.axis_index("circ")
    stator = lax.axis_index("sec") == 1
    sub, _ = iotas()
    slots = targets_ref.shape[-1]
    for d in range(targets_ref.shape[0]):
        for k in range(slots):
            live = (k < counts_ref[d, me]) & stator
            row = jnp.where(live, targets_ref[d, me, k], -1)
            w = jnp.broadcast_to(weights_ref[d * slots + k : d * slots + k + 1, :], (SUB, LANES))
            for h in range(2):
                placed_ref[d, k, SUB * h : SUB * (h + 1), :] = jnp.where(sub + SUB * h == row, w, 0.0)


def local_sums(lam_ref, couple_ref, near_ref, inv_ref=None):
    nv, na = lam_ref.shape[:2]
    sub, lane = iotas()
    for a in range(na):
        coef = []
        for half in range(2):
            rows = slice(SUB * half, SUB * (half + 1))
            c = [couple_ref[i, a, rows, :] for i in range(12)]
            if inv_ref is not None:
                total = c[0]
                for i in range(1, 12):
                    total = total + c[i]
                inv_ref[a, rows, :] = 1.0 / (1.0 + total)
            if half == 0:
                c[4] = jnp.where(sub >= 2, c[4], 0.0)
                c[5] = jnp.where(sub >= 1, c[5], 0.0)
            else:
                c[6] = jnp.where(sub < SUB - 1, c[6], 0.0)
                c[7] = jnp.where(sub < SUB - 2, c[7], 0.0)
            c[8] = jnp.where(lane >= 2, c[8], 0.0)
            c[9] = jnp.where(lane >= 1, c[9], 0.0)
            c[10] = jnp.where(lane < LANES - 1, c[10], 0.0)
            c[11] = jnp.where(lane < LANES - 2, c[11], 0.0)
            coef.append(c)
        for v in range(nv):
            x = [lam_ref[v, a, SUB * h : SUB * (h + 1), :] for h in range(2)]
            moved = {o: [down(x[h], -o) for h in range(2)] for o in (-2, -1, 1, 2)}
            for half in range(2):
                rows = slice(SUB * half, SUB * (half + 1))
                c = coef[half]
                total = None
                for i, o in enumerate((-2, -1, 1, 2)):
                    if 0 <= a + o < na:
                        term = c[i] * lam_ref[v, a + o, rows, :]
                        total = term if total is None else total + term
                for i, o in enumerate((-2, -1, 1, 2)):
                    m = moved[o]
                    if o < 0:
                        y = m[0] if half == 0 else jnp.where(sub >= -o, m[1], m[0])
                    else:
                        y = m[1] if half == 1 else jnp.where(sub < SUB - o, m[0], m[1])
                    total = total + c[4 + i] * y
                for i, o in enumerate((-2, -1, 1, 2)):
                    total = total + c[8 + i] * along(x[half], -o)
                near_ref[v, a, rows, :] = total


def work_kernel(*refs):
    lam_ref, couple_in, jac_in, src_in, weights_in, targets_in, counts_in = refs[:7]
    couple_ref, jac_ref, src_ref, near_ref, inv_ref, placed_ref = refs[7:13]
    weights_ref, targets_ref, counts_ref, big, small = refs[13:]
    wide = [
        pltpu.make_async_copy(couple_in, couple_ref, big.at[0]),
        pltpu.make_async_copy(src_in, src_ref, big.at[1]),
    ] + [
        pltpu.make_async_copy(jac_in.at[s], jac_ref.at[s], big.at[2 + s])
        for s in range(jac_ref.shape[0])
    ]
    slim = [
        pltpu.make_async_copy(weights_in, weights_ref, small.at[0]),
        pltpu.make_async_copy(targets_in, targets_ref, small.at[1]),
        pltpu.make_async_copy(counts_in, counts_ref, small.at[2]),
    ]
    for copy in slim + wide:
        copy.start()
    for copy in slim:
        copy.wait()
    place_weights(targets_ref, counts_ref, weights_ref, placed_ref)
    wide[0].wait()
    local_sums(lam_ref, couple_ref, near_ref, inv_ref)
    for copy in wide[1:]:
        copy.wait()


def local_kernel(lam_ref, couple_ref, _, near_ref):
    local_sums(lam_ref, couple_ref, near_ref)


def relay_kernel(*refs):
    cols_ref, *refs = refs
    routes = len(refs) // 2
    share = shares(routes)
    for n, (tile_ref, out_ref) in enumerate(zip(refs[:routes], refs[routes:])):
        half = tile_ref.shape[0] // 2
        out_ref[share : share + half, :] = tile_ref[half:, :]
        if share * n < cols_ref.shape[0]:
            out_ref[:share, :] = cols_ref[share * n : share * (n + 1), :]


def shares(routes):
    return SUB * max(1, 4 // routes)


def finish_kernel(faces, last, *refs):
    near_ref, couple_ref, jac_ref, src_ref, inv_ref, ahead_ref, back_ref, across_ref = refs[:8]
    if faces:
        relayed, direct = refs[8 : 8 + faces], refs[8 + faces : 8 + 2 * faces]
        placed_ref, out_ref, rhs_ref, *rest = refs[8 + 2 * faces :]
        share = shares(faces)
        mate_at = lambda at: relayed[at // share][at % share : at % share + SUB, :]
    else:
        mate_ref, out_ref, *rest = refs[8:]
        mate_at = lambda at: mate_ref[at : at + SUB, :]
    nv, na = near_ref.shape[:2]
    sub, lane = iotas()
    circs, rads = lax.axis_size("circ"), lax.axis_size("rad")
    me, rad = lax.axis_index("circ"), lax.axis_index("rad")
    even = me % 2 == 0
    has_low = rad > 0
    has_high = rad < rads - 1

    low_rows, high_rows = [], []
    for g in range(nv * na // 4):
        rows = slice(SUB * g, SUB * (g + 1))
        x, y = ahead_ref[rows, :], back_ref[rows, :]
        low_rows.append(jnp.where(even, x, y))
        high_rows.append(jnp.where(even, y, x))

    wide, slim = {}, {}
    for part in range(nv * na // GROUP):
        for half in range(2):
            at = SUB * (2 * part + half)
            x, y = mate_at(at), across_ref[at : at + SUB, :]
            right = along(jnp.where(even, x, y), -2)
            left = along(jnp.where(even, y, x), 2)
            wide[part, half] = jnp.where(lane % 4 < 2, right, left)
            slim[part, half] = jnp.where(lane % 4 < 2, along(right, 1), along(left, -1))

    packer = None if last else Packer(na, nv)
    for a in range(na):
        for half in range(2):
            rows = slice(SUB * half, SUB * (half + 1))
            c = [couple_ref[i, a, rows, :] for i in range(4, 12)]
            if half == 0:
                far = jnp.where((sub < 2) & has_low, c[0], 0.0)
                nigh = jnp.where((sub < 1) & has_low, c[1], 0.0)
            else:
                far = jnp.where((sub >= SUB - 2) & has_high, c[3], 0.0)
                nigh = jnp.where((sub >= SUB - 1) & has_high, c[2], 0.0)
            outer = jnp.where(lane < 2, c[4], jnp.where(lane >= LANES - 2, c[7], 0.0))
            inner = jnp.where(lane < 1, c[5], jnp.where(lane >= LANES - 1, c[6], 0.0))
            near = []
            for v in range(nv):
                k = v * na + a
                j = k % 4
                if half == 0:
                    m = low_rows[k // 4]
                    y2, y1 = down(m, -2 * j), down(m, -2 * j - 1)
                else:
                    m = high_rows[k // 4]
                    y2, y1 = down(m, 6 - 2 * j), down(m, 7 - 2 * j)
                spot = 4 * (k % GROUP)
                key = (k // GROUP, half)
                total = near_ref[v, a, rows, :] + (far * y2 + nigh * y1)
                total = total + outer * along(wide[key], LANES - 2 - spot)
                total = total + inner * along(slim[key], LANES - 2 - spot)
                near.append(total)
            inv = inv_ref[a, rows, :]
            for s in range(nv):
                acc = src_ref[s, a, rows, :]
                if faces and a < 2:
                    sources = [(ref, 0, me - 2 * n) for n, ref in enumerate(direct)]
                    sources += [(ref, share, me + 1 - 2 * (me % 2) - 2 * n) for n, ref in enumerate(relayed)]
                    for tile_ref, start, donor in sources:
                        donor = lax.rem(donor + circs, circs)
                        for t in range(placed_ref.shape[1]):
                            at = start + (t * nv + s) * 2 + a
                            tile = jnp.broadcast_to(tile_ref[at : at + 1, :], (SUB, LANES))
                            acc = acc + placed_ref[donor, t, rows, :] * tile
                if faces:
                    rhs_ref[s, a, rows, :] = acc
                for b in range(nv):
                    acc = acc + jac_ref[s, b, a, rows, :] * near[b]
                x = acc * inv
                out_ref[s, a, rows, :] = x
                if packer is not None:
                    packer.add(s, a, half, x)
    if packer is not None:
        packer.write(*rest)


def call(kernel, name, outs, args, specs=None, scratch=(), us=1):
    vmem = pl.BlockSpec(memory_space=pltpu.VMEM)
    return pl.pallas_call(
        kernel,
        out_shape=outs,
        in_specs=[vmem] * len(args) if specs is None else specs,
        out_specs=[vmem] * len(outs),
        scratch_shapes=list(scratch),
        compiler_params=PARAMS,
        cost_estimate=pl.CostEstimate(
            flops=us * 1_000_000, bytes_accessed=us * 3_000_000, transcendentals=0
        ),
        name=name,
    )(*args)


def solution(mesh):
    route = routes(mesh)
    vmem = lambda *shape: pltpu.VMEM(shape, jnp.float32)
    inside = pl.BlockSpec(memory_space=pltpu.VMEM)
    outside = pl.BlockSpec(memory_space=pltpu.HBM)
    far = lambda x: pltpu.with_memory_space_constraint(x, pltpu.HBM)
    unread = pl.BlockSpec(memory_space=pl.ANY)

    def sent(x, pairs):
        return lax.ppermute(x, AXES, pairs)

    def per_device(adjoint, source, jacobian, couple, donor_row, target_row, tile_count, weights):
        nv, na, nr, nc = adjoint.shape[1:]
        donors, slots = donor_row.shape[2:]
        edges = [vmem(2 * nv * na, nc), vmem(2 * nv * na, nc), vmem(4 * SUB, nc)]
        count = len(route["faces"])
        ahead, back, cols, *tiles, lam = call(
            pack_kernel, "pack",
            edges + [vmem(4 * slots * nv, nc)] * count + [vmem(nv, na, nr, nc)],
            [far(adjoint[0]), far(donor_row[0])], [outside] * 2,
            [pltpu.SMEM(donor_row.shape[1:], jnp.int32), pltpu.SemaphoreType.DMA((nv + 1,))],
        )
        rhs = None
        for sweep in range(SWEEPS):
            first, last = sweep == 0, sweep == SWEEPS - 1
            if first:
                tiles = [sent(x, pairs) for x, pairs in zip(tiles, route["faces"])]
            ahead = sent(ahead, route["ahead"])
            back = sent(back, route["back"])
            across = sent(cols, route["across"])
            if first:
                relayed = call(
                    relay_kernel, "relay", [vmem(shares(count) + 2 * slots * nv, nc)] * count, [cols, *tiles]
                )
                relayed = [sent(x, route["mate"]) for x in relayed]
                cpl, jac, rhs, near, inv, placed = call(
                    work_kernel, "work",
                    [vmem(12, na, nr, nc), vmem(nv, nv, na, nr, nc), vmem(nv, na, nr, nc),
                     vmem(nv, na, nr, nc), vmem(na, nr, nc), vmem(donors, slots, nr, nc)],
                    [lam, *map(far, (couple[0], jacobian[0], source[0], weights.reshape(-1, nc),
                                     target_row[0], tile_count[0]))],
                    [inside] + [outside] * 6,
                    [pltpu.VMEM((donors * slots, nc), jnp.float32),
                     pltpu.SMEM(target_row.shape[1:], jnp.int32), pltpu.SMEM(tile_count.shape[1:], jnp.int32),
                     pltpu.SemaphoreType.DMA((2 + nv,)), pltpu.SemaphoreType.DMA((3,))],
                )
                extra = relayed + tiles + [placed]
            else:
                mate = sent(cols, route["mate"])
                extra = [mate]
                near = call(
                    local_kernel, f"local{sweep}", [vmem(nv, na, nr, nc)],
                    [lam, cpl, mate], [inside, inside, unread],
                )[0]
            if last:
                outs = [jax.ShapeDtypeStruct((nv, na, nr, nc), jnp.float32)]
            else:
                outs = [vmem(nv, na, nr, nc)] * (2 if first else 1) + edges
            lam, *more = call(
                lambda *refs, n=count if first else 0, last=last: finish_kernel(n, last, *refs),
                f"finish{sweep}", outs, [near, cpl, jac, rhs, inv, ahead, back, across] + extra,
            )
            if first:
                rhs, *more = more
            if not last:
                ahead, back, cols = more
        return lam[None]

    in_specs = (
        P("sec", None, None, "rad", "circ"),
        P("sec", None, None, "rad", "circ"),
        P("sec", None, None, None, "rad", "circ"),
        P("sec", None, None, "rad", "circ"),
        P("rad", None, None, None),
        P("rad", None, None, None),
        P("rad", None, None),
        P("rad", None, "circ", None, None),
    )
    out_specs = P("sec", None, None, "rad", "circ")
    return jax.shard_map(
        per_device, mesh=mesh, in_specs=in_specs, out_specs=out_specs, check_vma=False
    )
```

```python
import jax
import jax.numpy as jnp
from jax import lax
from jax.experimental import pallas as pl
from jax.experimental.pallas import tpu as pltpu
from jax.sharding import PartitionSpec as P

SWEEPS = 3
AXES = ("sec", "circ", "rad")
SUB, LANES = 8, 128
GROUP = 20
EARLY = 3
PARAMS = pltpu.CompilerParams(vmem_limit_bytes=16 * 1024 * 1024)


def routes(mesh):
    secs, circs, rads = (mesh.shape[a] for a in AXES)

    def pairs(target):
        flat = lambda s, c, r: (s * circs + c) * rads + r
        return [
            (flat(s, c, r), flat(*target(s, c, r)))
            for s in range(secs)
            for c in range(circs)
            for r in range(rads)
        ]

    def swap(s, c, r, odd):
        q = r + 1 if (r + odd) % 2 == 0 else r - 1
        return (s, c, q) if 0 <= q < rads else (s, c ^ 1, r)

    return {
        "ahead": pairs(lambda s, c, r: swap(s, c, r, 0)),
        "back": pairs(lambda s, c, r: swap(s, c, r, 1)),
        "mate": pairs(lambda s, c, r: (s, c ^ 1, r)),
        "across": pairs(lambda s, c, r: (s, (c - 1 if c % 2 == 0 else c + 1) % circs, r)),
        "faces": [
            pairs(lambda s, c, r: (1, (c + k) % circs, r) if s == 0 else (0, (c - k) % circs, r))
            for k in range(0, circs, 2)
        ],
    }


def iotas():
    sub = lax.broadcasted_iota(jnp.int32, (SUB, LANES), 0)
    lane = lax.broadcasted_iota(jnp.int32, (SUB, LANES), 1)
    return sub, lane


def down(x, by):
    return pltpu.roll(x, by % SUB, 0) if by % SUB else x


def along(x, by):
    return pltpu.roll(x, by % LANES, 1) if by % LANES else x


class Packer:
    def __init__(self, na, nv):
        self.sub, self.lane = iotas()
        self.na = na
        self.low, self.high, self.cols = {}, {}, {}

    def put(self, book, key, keep, x):
        book[key] = jnp.where(keep, x, book[key]) if key in book else x

    def add(self, v, a, half, x):
        k = v * self.na + a
        group, j = k // 4, k % 4
        inside = (self.sub >= 2 * j) & (self.sub < 2 * j + 2)
        if half == 0:
            self.put(self.low, group, inside, down(x, 2 * j))
        else:
            self.put(self.high, group, inside, down(x, 2 * j + 2))
        spot = 4 * (k % GROUP)
        inside = (self.lane >= spot) & (self.lane < spot + 4)
        self.put(self.cols, (k // GROUP, half), inside, along(x, spot + 2))

    def write(self, ahead_ref, back_ref, across_ref, mate_refs):
        even = lax.axis_index("rad") % 2 == 0
        for g in range(len(self.low)):
            rows = slice(SUB * g, SUB * (g + 1))
            ahead_ref[rows, :] = jnp.where(even, self.high[g], self.low[g])
            back_ref[rows, :] = jnp.where(even, self.low[g], self.high[g])
        even = lax.axis_index("circ") % 2 == 0
        for half in range(2):
            x, y = self.cols[0, half], self.cols[1, half]
            right = jnp.where(self.lane % 4 < 2, x, along(y, 2))
            left = jnp.where(self.lane % 4 < 2, along(y, -2), x)
            rows = slice(SUB * half, SUB * (half + 1))
            across_ref[rows, :] = jnp.where(even, left, right)
            mate_refs[half][...] = jnp.where(even, right, left)


def pack_kernel(adjoint_ref, donors_in, couple_in, src_in, jac_in, *refs):
    ahead_ref, back_ref, across_ref, mate_ref, lam_ref, couple_ref, src_ref, jac_ref = refs[:8]
    *tile_refs, donors_ref, sems, more_sems = refs[8:]
    nv, na, nr, _ = lam_ref.shape
    listed = pltpu.make_async_copy(donors_in, donors_ref, sems.at[nv])
    listed.start()
    copies = [pltpu.make_async_copy(adjoint_ref.at[v], lam_ref.at[v], sems.at[v]) for v in range(nv)]
    later = [
        pltpu.make_async_copy(couple_in, couple_ref, more_sems.at[0]),
        pltpu.make_async_copy(src_in, src_ref, more_sems.at[1]),
        pltpu.make_async_copy(jac_in.at[: jac_ref.shape[0]], jac_ref, more_sems.at[2]),
    ]
    for copy in copies + later:
        copy.start()
    packer = Packer(na, nv)
    for v in range(nv):
        copies[v].wait()
        for a in range(na):
            for half in range(2):
                packer.add(v, a, half, lam_ref[v, a, SUB * half : SUB * (half + 1), :])
    packer.write(ahead_ref, back_ref, across_ref, [mate_ref.at[:SUB], mate_ref.at[SUB:]])
    listed.wait()
    me, circs, slots = lax.axis_index("circ"), donors_ref.shape[1], donors_ref.shape[2]
    for n, tile_ref in enumerate(tile_refs):
        reader = lax.rem(me + 2 * n, circs)
        for part, to in enumerate((reader, reader + 1 - 2 * (reader % 2))):
            for k in range(slots):
                row = jnp.clip(donors_ref[me, to, k], 0, nr - 1)
                for v in range(nv):
                    for a in range(2):
                        at = ((part * slots + k) * nv + v) * 2 + a
                        tile_ref[at : at + 1, :] = lam_ref[v, na - 2 + a, pl.ds(row, 1), :]
    for copy in later:
        copy.wait()


def place_weights(targets_ref, counts_ref, weights_ref, placed_ref):
    me = lax.axis_index("circ")
    stator = lax.axis_index("sec") == 1
    sub, _ = iotas()
    slots = targets_ref.shape[-1]
    for d in range(targets_ref.shape[0]):
        for k in range(slots):
            live = (k < counts_ref[d, me]) & stator
            row = jnp.where(live, targets_ref[d, me, k], -1)
            w = jnp.broadcast_to(weights_ref[d * slots + k : d * slots + k + 1, :], (SUB, LANES))
            for h in range(2):
                placed_ref[d, k, SUB * h : SUB * (h + 1), :] = jnp.where(sub + SUB * h == row, w, 0.0)


def local_sums(lam_ref, couple_ref, near_ref, inv_ref=None):
    nv, na = lam_ref.shape[:2]
    sub, lane = iotas()
    for a in range(na):
        coef = []
        for half in range(2):
            rows = slice(SUB * half, SUB * (half + 1))
            c = [couple_ref[i, a, rows, :] for i in range(12)]
            if inv_ref is not None:
                total = c[0]
                for i in range(1, 12):
                    total = total + c[i]
                inv_ref[a, rows, :] = 1.0 / (1.0 + total)
            if half == 0:
                c[4] = jnp.where(sub >= 2, c[4], 0.0)
                c[5] = jnp.where(sub >= 1, c[5], 0.0)
            else:
                c[6] = jnp.where(sub < SUB - 1, c[6], 0.0)
                c[7] = jnp.where(sub < SUB - 2, c[7], 0.0)
            c[8] = jnp.where(lane >= 2, c[8], 0.0)
            c[9] = jnp.where(lane >= 1, c[9], 0.0)
            c[10] = jnp.where(lane < LANES - 1, c[10], 0.0)
            c[11] = jnp.where(lane < LANES - 2, c[11], 0.0)
            coef.append(c)
        for v in range(nv):
            x = [lam_ref[v, a, SUB * h : SUB * (h + 1), :] for h in range(2)]
            moved = {o: [down(x[h], -o) for h in range(2)] for o in (-2, -1, 1, 2)}
            for half in range(2):
                rows = slice(SUB * half, SUB * (half + 1))
                c = coef[half]
                total = None
                for i, o in enumerate((-2, -1, 1, 2)):
                    if 0 <= a + o < na:
                        term = c[i] * lam_ref[v, a + o, rows, :]
                        total = term if total is None else total + term
                for i, o in enumerate((-2, -1, 1, 2)):
                    m = moved[o]
                    if o < 0:
                        y = m[0] if half == 0 else jnp.where(sub >= -o, m[1], m[0])
                    else:
                        y = m[1] if half == 1 else jnp.where(sub < SUB - o, m[0], m[1])
                    total = total + c[4 + i] * y
                for i, o in enumerate((-2, -1, 1, 2)):
                    total = total + c[8 + i] * along(x[half], -o)
                near_ref[v, a, rows, :] = total


def work_kernel(*refs):
    lam_ref, couple_ref, jac_in, weights_in, targets_in, counts_in = refs[:6]
    jac_ref, near_ref, inv_ref, placed_ref = refs[6:10]
    weights_ref, targets_ref, counts_ref, sems = refs[10:]
    count = jac_ref.shape[0]
    wide = pltpu.make_async_copy(jac_in.at[jac_in.shape[0] - count :], jac_ref, sems.at[0])
    slim = [
        pltpu.make_async_copy(weights_in, weights_ref, sems.at[1]),
        pltpu.make_async_copy(targets_in, targets_ref, sems.at[2]),
        pltpu.make_async_copy(counts_in, counts_ref, sems.at[3]),
    ]
    for copy in slim + [wide]:
        copy.start()
    local_sums(lam_ref, couple_ref, near_ref, inv_ref)
    for copy in slim:
        copy.wait()
    place_weights(targets_ref, counts_ref, weights_ref, placed_ref)
    wide.wait()


def local_kernel(lam_ref, couple_ref, near_ref):
    local_sums(lam_ref, couple_ref, near_ref)


def relay_kernel(*refs):
    cols_ref, *refs = refs
    routes = len(refs) // 2
    share = shares(routes)
    for n, (tile_ref, out_ref) in enumerate(zip(refs[:routes], refs[routes:])):
        half = tile_ref.shape[0] // 2
        out_ref[share : share + half, :] = tile_ref[half:, :]
        if share * n < cols_ref.shape[0]:
            out_ref[:share, :] = cols_ref[share * n : share * (n + 1), :]


def shares(routes):
    return SUB * max(1, 2 // routes)


def finish_kernel(faces, last, *refs):
    near_ref, couple_ref, jac_first, jac_rest, src_ref, inv_ref, ahead_ref, back_ref, across_ref = refs[:9]
    jac = lambda s: (jac_first, s) if s < jac_first.shape[0] else (jac_rest, s - jac_first.shape[0])
    if faces:
        relayed, direct = refs[9 : 9 + faces], refs[9 + faces : 9 + 2 * faces]
        placed_ref, out_ref, rhs_ref, *rest = refs[9 + 2 * faces :]
        share = shares(faces)
        mate_at = lambda at: relayed[at // share][at % share : at % share + SUB, :]
    else:
        mate_ref, out_ref, *rest = refs[9:]
        mate_at = lambda at: mate_ref[at : at + SUB, :]
    if last:
        result_ref, out_ref, sems = out_ref, *rest
        copies = []
    nv, na = near_ref.shape[:2]
    sub, lane = iotas()
    circs, rads = lax.axis_size("circ"), lax.axis_size("rad")
    me, rad = lax.axis_index("circ"), lax.axis_index("rad")
    has_low = rad > 0
    has_high = rad < rads - 1

    low_rows, high_rows = [], []
    for g in range(nv * na // 4):
        rows = slice(SUB * g, SUB * (g + 1))
        x, y = ahead_ref[rows, :], back_ref[rows, :]
        low_rows.append(jnp.where(rad % 2 == 0, y, x))
        high_rows.append(jnp.where(rad % 2 == 0, x, y))

    wide, slim = {}, {}
    for half in range(2):
        at = SUB * half
        x, y = mate_at(at), across_ref[at : at + SUB, :]
        right = jnp.where(me % 2 == 0, x, y)
        left = jnp.where(me % 2 == 0, y, x)
        for part, (r, l) in enumerate(((along(right, -2), along(left, 2)), (right, left))):
            wide[part, half] = jnp.where(lane % 4 < 2, r, l)
            slim[part, half] = jnp.where(lane % 4 < 2, along(r, 1), along(l, -1))

    packer = None if last else Packer(na, nv)
    for a in range(na):
        for half in range(2):
            rows = slice(SUB * half, SUB * (half + 1))
            c = [couple_ref[i, a, rows, :] for i in range(4, 12)]
            if half == 0:
                far = jnp.where((sub < 2) & has_low, c[0], 0.0)
                nigh = jnp.where((sub < 1) & has_low, c[1], 0.0)
            else:
                far = jnp.where((sub >= SUB - 2) & has_high, c[3], 0.0)
                nigh = jnp.where((sub >= SUB - 1) & has_high, c[2], 0.0)
            outer = jnp.where(lane < 2, c[4], jnp.where(lane >= LANES - 2, c[7], 0.0))
            inner = jnp.where(lane < 1, c[5], jnp.where(lane >= LANES - 1, c[6], 0.0))
            near = []
            for v in range(nv):
                k = v * na + a
                j = k % 4
                if half == 0:
                    m = low_rows[k // 4]
                    y2, y1 = down(m, -2 * j), down(m, -2 * j - 1)
                else:
                    m = high_rows[k // 4]
                    y2, y1 = down(m, 6 - 2 * j), down(m, 7 - 2 * j)
                spot = 4 * (k % GROUP)
                key = (k // GROUP, half)
                total = near_ref[v, a, rows, :] + (far * y2 + nigh * y1)
                total = total + outer * along(wide[key], LANES - 2 - spot)
                total = total + inner * along(slim[key], LANES - 2 - spot)
                near.append(total)
            inv = inv_ref[a, rows, :]
            for s in range(nv):
                acc = src_ref[s, a, rows, :]
                if faces and a < 2:
                    sources = [(ref, 0, me - 2 * n) for n, ref in enumerate(direct)]
                    sources += [(ref, share, me + 1 - 2 * (me % 2) - 2 * n) for n, ref in enumerate(relayed)]
                    for tile_ref, start, donor in sources:
                        donor = lax.rem(donor + circs, circs)
                        for t in range(placed_ref.shape[1]):
                            at = start + (t * nv + s) * 2 + a
                            tile = jnp.broadcast_to(tile_ref[at : at + 1, :], (SUB, LANES))
                            acc = acc + placed_ref[donor, t, rows, :] * tile
                if faces:
                    rhs_ref[s, a, rows, :] = acc
                jac_ref, row = jac(s)
                for b in range(nv):
                    acc = acc + jac_ref[row, b, a, rows, :] * near[b]
                x = acc * inv
                out_ref[s, a, rows, :] = x
                if packer is not None:
                    packer.add(s, a, half, x)
        if last:
            copy = pltpu.make_async_copy(out_ref.at[:, a], result_ref.at[:, a], sems.at[a])
            copy.start()
            copies.append(copy)
    if last:
        for copy in copies:
            copy.wait()
    else:
        ahead_to, back_to, across_to, mate_to = rest
        packer.write(ahead_to, back_to, across_to, [mate_to.at[:SUB], mate_to.at[SUB:]])


def call(kernel, name, outs, args, specs=None, scratch=(), us=1, out_specs=None):
    vmem = pl.BlockSpec(memory_space=pltpu.VMEM)
    return pl.pallas_call(
        kernel,
        out_shape=outs,
        in_specs=[vmem] * len(args) if specs is None else specs,
        out_specs=[vmem] * len(outs) if out_specs is None else out_specs,
        scratch_shapes=list(scratch),
        compiler_params=PARAMS,
        cost_estimate=pl.CostEstimate(
            flops=us * 1_000_000, bytes_accessed=us * 3_000_000, transcendentals=0
        ),
        name=name,
    )(*args)


def solution(mesh):
    route = routes(mesh)
    vmem = lambda *shape: pltpu.VMEM(shape, jnp.float32)
    inside = pl.BlockSpec(memory_space=pltpu.VMEM)
    outside = pl.BlockSpec(memory_space=pltpu.HBM)
    far = lambda x: pltpu.with_memory_space_constraint(x, pltpu.HBM)

    def sent(x, pairs):
        return lax.ppermute(x, AXES, pairs)

    def per_device(adjoint, source, jacobian, couple, donor_row, target_row, tile_count, weights):
        nv, na, nr, nc = adjoint.shape[1:]
        donors, slots = donor_row.shape[2:]
        count = len(route["faces"])
        sides = 2 * nv * na
        edges = lambda across: [vmem(sides + SUB, nc), vmem(sides, nc), vmem(across, nc), vmem(nr, nc)]
        early = EARLY
        ahead, back, cross, cols, lam, cpl, rhs, jac_first, *tiles = call(
            pack_kernel, "pack",
            edges(sides - SUB) + [vmem(nv, na, nr, nc), vmem(12, na, nr, nc), vmem(nv, na, nr, nc),
                                  vmem(early, nv, na, nr, nc)] + [vmem(4 * slots * nv, nc)] * count,
            [far(adjoint[0]), far(donor_row[0]), far(couple[0]), far(source[0]), far(jacobian[0])], [outside] * 5,
            [pltpu.SMEM(donor_row.shape[1:], jnp.int32), pltpu.SemaphoreType.DMA((nv + 1,)),
             pltpu.SemaphoreType.DMA((3,))],
        )
        for sweep in range(SWEEPS):
            first, last = sweep == 0, sweep == SWEEPS - 1
            if first:
                tiles = [sent(x, pairs) for x, pairs in zip(tiles, route["faces"])]
            ahead = sent(ahead, route["ahead"])
            back = sent(back, route["back"])
            across = sent(cross, route["across"])
            if first:
                relayed = call(
                    relay_kernel, "relay", [vmem(shares(count) + 2 * slots * nv, nc)] * count, [cols, *tiles]
                )
                relayed = [sent(x, route["mate"]) for x in relayed]
                jac_rest, near, inv, placed = call(
                    work_kernel, "work",
                    [vmem(nv - early, nv, na, nr, nc), vmem(nv, na, nr, nc), vmem(na, nr, nc),
                     vmem(donors, slots, nr, nc)],
                    [lam, cpl, *map(far, (jacobian[0], weights.reshape(-1, nc), target_row[0], tile_count[0]))],
                    [inside] * 2 + [outside] * 4,
                    [pltpu.VMEM((donors * slots, nc), jnp.float32),
                     pltpu.SMEM(target_row.shape[1:], jnp.int32), pltpu.SMEM(tile_count.shape[1:], jnp.int32),
                     pltpu.SemaphoreType.DMA((4,))],
                )
                extra = relayed + tiles + [placed]
            else:
                mate = sent(cols, route["mate"])
                extra = [mate]
                near = call(
                    local_kernel, f"local{sweep}", [vmem(nv, na, nr, nc)],
                    [lam, cpl],
                )[0]
            scratch, spaces = [], None
            if last:
                outs, spaces = [jax.ShapeDtypeStruct((nv, na, nr, nc), jnp.float32)], [outside]
                scratch = [pltpu.VMEM((nv, na, nr, nc), jnp.float32), pltpu.SemaphoreType.DMA((na,))]
            else:
                outs = [vmem(nv, na, nr, nc)] * (2 if first else 1) + edges(nr + SUB)
            lam, *more = call(
                lambda *refs, n=count if first else 0, last=last: finish_kernel(n, last, *refs),
                f"finish{sweep}", outs,
                [near, cpl, jac_first, jac_rest, rhs, inv, ahead, back, across] + extra,
                None, scratch, 1, spaces,
            )
            if first:
                rhs, *more = more
            if not last:
                ahead, back, cross, cols = more
        return lam[None]

    in_specs = (
        P("sec", None, None, "rad", "circ"),
        P("sec", None, None, "rad", "circ"),
        P("sec", None, None, None, "rad", "circ"),
        P("sec", None, None, "rad", "circ"),
        P("rad", None, None, None),
        P("rad", None, None, None),
        P("rad", None, None),
        P("rad", None, "circ", None, None),
    )
    out_specs = P("sec", None, None, "rad", "circ")
    return jax.shard_map(
        per_device, mesh=mesh, in_specs=in_specs, out_specs=out_specs, check_vma=False
    )
```

```python
import functools

import jax
import jax.numpy as jnp
from jax import lax
from jax.experimental import pallas as pl
from jax.experimental.pallas import tpu as pltpu
from jax.sharding import PartitionSpec as P

SWEEPS = 3
AXES = ("sec", "circ", "rad")
SUB, LANES = 8, 128
PARAMS = pltpu.CompilerParams(vmem_limit_bytes=16 * 1024 * 1024)


def routes(mesh):
    secs, circs, rads = (mesh.shape[a] for a in AXES)

    def pairs(target):
        flat = lambda s, c, r: (s * circs + c) * rads + r
        return [
            (flat(s, c, r), flat(*target(s, c, r)))
            for s in range(secs)
            for c in range(circs)
            for r in range(rads)
        ]

    def swap(s, c, r, odd):
        q = r + 1 if (r + odd) % 2 == 0 else r - 1
        return (s, c, q) if 0 <= q < rads else (s, c ^ 1, r)

    return {
        "ahead": pairs(lambda s, c, r: swap(s, c, r, 0)),
        "back": pairs(lambda s, c, r: swap(s, c, r, 1)),
        "mate": pairs(lambda s, c, r: (s, c ^ 1, r)),
        "across": pairs(lambda s, c, r: (s, (c - 1 if c % 2 == 0 else c + 1) % circs, r)),
        "faces": [
            pairs(lambda s, c, r: (1, (c + k) % circs, r) if s == 0 else (0, (c - k) % circs, r))
            for k in range(0, circs, 2)
        ],
    }


def iotas():
    sub = lax.broadcasted_iota(jnp.int32, (SUB, LANES), 0)
    lane = lax.broadcasted_iota(jnp.int32, (SUB, LANES), 1)
    return sub, lane


def down(x, by):
    return pltpu.roll(x, by % SUB, 0) if by % SUB else x


def along(x, by):
    return pltpu.roll(x, by % LANES, 1) if by % LANES else x


def half_rows(half):
    return slice(SUB * half, SUB * (half + 1))


def slot(v, a, na):
    return v % 2, 4 * (na * (v // 2) + a) + 2 * (v % 2)


class Packer:
    def __init__(self, na, nv):
        self.sub, self.lane = iotas()
        self.na = na
        self.low, self.high, self.cols = {}, {}, {}

    def put(self, book, key, keep, x):
        book[key] = jnp.where(keep, x, book[key]) if key in book else x

    def add(self, v, a, half, x):
        k = v * self.na + a
        group, j = k // 4, k % 4
        inside = (self.sub >= 2 * j) & (self.sub < 2 * j + 2)
        if half == 0:
            self.put(self.low, group, inside, down(x, 2 * j))
        else:
            self.put(self.high, group, inside, down(x, 2 * j + 2))
        part, spot = slot(v, a, self.na)
        inside = (self.lane >= spot) & (self.lane < spot + 4)
        self.put(self.cols, (part, half), inside, along(x, spot + 2))

    def write(self, ahead_ref, back_ref, across_ref, mate_refs):
        even = lax.axis_index("rad") % 2 == 0
        for g in range(len(self.low)):
            rows = slice(SUB * g, SUB * (g + 1))
            ahead_ref[rows, :] = jnp.where(even, self.high[g], self.low[g])
            back_ref[rows, :] = jnp.where(even, self.low[g], self.high[g])
        even = lax.axis_index("circ") % 2 == 0
        for half in range(2):
            x, y = self.cols[0, half], self.cols[1, half]
            right = jnp.where(self.lane % 4 < 2, x, y)
            left = jnp.where(self.lane % 4 < 2, y, x)
            rows = slice(SUB * half, SUB * (half + 1))
            across_ref[rows, :] = jnp.where(even, left, right)
            mate_refs[half][...] = jnp.where(even, right, left)


def pack_kernel(lam_ref, ahead_ref, back_ref, across_ref, mate_ref):
    nv, na = lam_ref.shape[:2]
    packer = Packer(na, nv)
    for a in range(na):
        for v in range(nv):
            for half in range(2):
                packer.add(v, a, half, lam_ref[v, a, SUB * half : SUB * (half + 1), :])
    packer.write(ahead_ref, back_ref, across_ref, [mate_ref.at[:SUB], mate_ref.at[SUB:]])


def load_kernel(adjoint_ref, donors_in, couple_in, src_in, jac_in, targets_in, counts_in, weights_in, *refs):
    lam_ref, couple_ref, src_ref, jac_ref, placed_ref, inv_ref, cols_ref, rows_ref, *tile_refs = refs[:-5]
    donors_ref, targets_ref, counts_ref, weights_ref, sems = refs[-5:]
    nv, na, nr, _ = lam_ref.shape
    copies = [
        pltpu.make_async_copy(donors_in, donors_ref, sems.at[0]),
        pltpu.make_async_copy(adjoint_ref, lam_ref, sems.at[1]),
        pltpu.make_async_copy(targets_in, targets_ref, sems.at[2]),
        pltpu.make_async_copy(counts_in, counts_ref, sems.at[3]),
        pltpu.make_async_copy(weights_in, weights_ref, sems.at[4]),
        pltpu.make_async_copy(couple_in, couple_ref, sems.at[5]),
        pltpu.make_async_copy(src_in, src_ref, sems.at[6]),
    ]
    copies += [pltpu.make_async_copy(jac_in.at[s], jac_ref.at[s], sems.at[7 + s]) for s in range(nv)]
    for copy in copies:
        copy.start()
    copies[0].wait()
    copies[1].wait()
    me, circs, slots = lax.axis_index("circ"), donors_ref.shape[1], donors_ref.shape[2]
    for n, tile_ref in enumerate(tile_refs):
        reader = jnp.where(me + 2 * n >= circs, me + 2 * n - circs, me + 2 * n)
        for part, to in enumerate((reader, reader + 1 - 2 * (reader % 2))):
            for k in range(slots):
                row = jnp.clip(donors_ref[me, to, k], 0, nr - 1)
                for v in range(nv):
                    for a in range(2):
                        at = ((part * slots + k) * nv + v) * 2 + a
                        tile_ref[at : at + 1, :] = lam_ref[v, na - 2 + a, pl.ds(row, 1), :]
    for copy in copies[2:5]:
        copy.wait()
    place_weights(targets_ref, counts_ref, weights_ref, placed_ref)
    copies[5].wait()
    coefs_of(couple_ref, inv_ref, cols_ref, rows_ref)
    for copy in copies[6:]:
        copy.wait()


def place_weights(targets_ref, counts_ref, weights_ref, placed_ref):
    me = lax.axis_index("circ")
    stator = lax.axis_index("sec") == 1
    sub, _ = iotas()
    slots = targets_ref.shape[-1]
    for d in range(targets_ref.shape[0]):
        for k in range(slots):
            live = (k < counts_ref[d, me]) & stator
            row = jnp.where(live, targets_ref[d, me, k], -1)
            w = jnp.broadcast_to(weights_ref[d * slots + k : d * slots + k + 1, :], (SUB, LANES))
            for h in range(2):
                placed_ref[d, k, SUB * h : SUB * (h + 1), :] = jnp.where(sub + SUB * h == row, w, 0.0)


def inner_coefs(c, half, sub, lane):
    c = list(c)
    if half == 0:
        c[4] = jnp.where(sub >= 2, c[4], 0.0)
        c[5] = jnp.where(sub >= 1, c[5], 0.0)
    else:
        c[6] = jnp.where(sub < SUB - 1, c[6], 0.0)
        c[7] = jnp.where(sub < SUB - 2, c[7], 0.0)
    c[8] = jnp.where(lane >= 2, c[8], 0.0)
    c[9] = jnp.where(lane >= 1, c[9], 0.0)
    c[10] = jnp.where(lane < LANES - 1, c[10], 0.0)
    c[11] = jnp.where(lane < LANES - 2, c[11], 0.0)
    return c


def local_sums(lam_ref, a, coef, sub):
    nv, na = lam_ref.shape[:2]
    sums = []
    for v in range(nv):
        x = [lam_ref[v, a, half_rows(h), :] for h in range(2)]
        moved = {o: [down(x[h], -o) for h in range(2)] for o in (-2, -1, 1, 2)}
        both = []
        for half in range(2):
            c = coef[half]
            total = None
            for i, o in enumerate((-2, -1, 1, 2)):
                if 0 <= a + o < na:
                    term = c[i] * lam_ref[v, a + o, half_rows(half), :]
                    total = term if total is None else total + term
            for i, o in enumerate((-2, -1, 1, 2)):
                m = moved[o]
                if o < 0:
                    y = m[0] if half == 0 else jnp.where(sub >= -o, m[1], m[0])
                else:
                    y = m[1] if half == 1 else jnp.where(sub < SUB - o, m[0], m[1])
                total = total + c[4 + i] * y
            for i, o in enumerate((-2, -1, 1, 2)):
                total = total + c[8 + i] * along(x[half], -o)
            both.append(total)
        sums.append(both)
    return sums


class Gather:
    def __init__(self, sub, lane):
        self.sub, self.lane = sub, lane
        self.got = {}

    def put(self, key, keep, x):
        self.got[key] = jnp.where(keep, x, self.got[key]) if key in self.got else x

    def cols(self, name, half, a, x):
        inside = (self.lane >= 4 * a) & (self.lane < 4 * a + 4)
        self.put((name, half), inside, along(x, 4 * a + 2))

    def rows(self, name, half, a, x):
        j = a % 4
        inside = (self.sub >= 2 * j) & (self.sub < 2 * j + 2)
        self.put((name, a // 4), inside, down(x, 2 * j + 2 * half))


def coefs_of(couple_ref, inv_ref, cols_ref, rows_ref):
    na = couple_ref.shape[1]
    sub, lane = iotas()
    rad = lax.axis_index("rad")
    has_low, has_high = rad > 0, rad < lax.axis_size("rad") - 1
    gather = Gather(sub, lane)
    for a in range(na):
        for half in range(2):
            c = [couple_ref[i, a, half_rows(half), :] for i in range(12)]
            total = c[0]
            for i in range(1, 12):
                total = total + c[i]
            inv_ref[a, half_rows(half), :] = 1.0 / (1.0 + total)
            gather.cols("outer", half, a, jnp.where(lane < 2, c[8], jnp.where(lane >= LANES - 2, c[11], 0.0)))
            gather.cols("inner", half, a, jnp.where(lane < 1, c[9], jnp.where(lane >= LANES - 1, c[10], 0.0)))
            if half == 0:
                gather.rows("low far", 0, a, jnp.where(has_low, c[4], 0.0))
                gather.rows("low nigh", 0, a, jnp.where(has_low & (sub < 1), c[5], 0.0))
            else:
                gather.rows("high far", 1, a, jnp.where(has_high, c[7], 0.0))
                gather.rows("high nigh", 1, a, jnp.where(has_high & (sub >= SUB - 1), c[6], 0.0))
    for i, name in enumerate(("outer", "inner")):
        for half in range(2):
            cols_ref[i, half_rows(half), :] = gather.got[name, half]
    for i, name in enumerate(("low far", "low nigh", "high far", "high nigh")):
        for q in range(na // 4):
            rows_ref[i, half_rows(q), :] = gather.got[name, q]


def work_kernel(lam_ref, couple_ref, near_ref):
    sub, lane = iotas()
    for a in range(lam_ref.shape[1]):
        coef = [
            inner_coefs([couple_ref[i, a, half_rows(h), :] for i in range(12)], h, sub, lane) for h in range(2)
        ]
        for v, both in enumerate(local_sums(lam_ref, a, coef, sub)):
            for half, x in enumerate(both):
                near_ref[v, a, half_rows(half), :] = x


def donor_at(at):
    return jnp.where(at < 0, at + lax.axis_size("circ"), at)


def add_tiles(x, sources, placed_ref, s, a, half, nv):
    for tile_ref, start, donor in sources:
        for t in range(placed_ref.shape[1]):
            at = start + (t * nv + s) * 2 + a
            tile = jnp.broadcast_to(tile_ref[at : at + 1, :], (SUB, LANES))
            x = x + placed_ref[donor, t, half_rows(half), :] * tile
    return x


def local_kernel(prepare, lam_ref, couple_ref, jac_ref, rhs_ref, inv_ref, base_ref, *edge_refs):
    nv, na = lam_ref.shape[:2]
    sub, lane = iotas()
    gathers = {}
    for a in range(na):
        coef = [
            inner_coefs([couple_ref[i, a, half_rows(h), :] for i in range(12)], h, sub, lane) for h in range(2)
        ]
        near = local_sums(lam_ref, a, coef, sub)
        for half in range(2):
            inv = inv_ref[a, half_rows(half), :]
            for s in range(nv):
                acc = rhs_ref[s, a, half_rows(half), :]
                for b in range(nv):
                    m = jac_ref[s, b, a, half_rows(half), :]
                    acc = acc + m * near[b][half]
                    if prepare:
                        m = m * inv
                        gather = gathers.setdefault((s, b), Gather(sub, lane))
                        gather.cols("cols", half, a, m)
                        gather.rows("high" if half else "low", half, a, m)
                base_ref[s, a, half_rows(half), :] = acc * inv
    if prepare:
        cols_ref, low_ref, high_ref = edge_refs
        for (s, b), gather in gathers.items():
            for half in range(2):
                cols_ref[s, b, half_rows(half), :] = gather.got["cols", half]
            for q in range(na // 4):
                low_ref[s, b, half_rows(q), :] = gather.got["low", q]
                high_ref[s, b, half_rows(q), :] = gather.got["high", q]


def relay_kernel(first, cols_ref, tile_ref, out_ref, *, share):
    half = out_ref.shape[0] - share
    out_ref[share:, :] = tile_ref[half : 2 * half, :]
    if first < cols_ref.shape[0]:
        out_ref[:share, :] = cols_ref[first : first + share, :]


def shares(routes):
    return SUB * max(1, 2 // routes)


def halo_sums(nv, na, ahead_ref, back_ref, across_ref, mate_at, cols_ref, rows_ref):
    sub, lane = iotas()
    me, rad = lax.axis_index("circ"), lax.axis_index("rad")
    out = []
    right, left = [], []
    for half in range(2):
        x, y = mate_at(half), across_ref[half_rows(half), :]
        right.append(jnp.where(me % 2 == 0, x, y))
        left.append(jnp.where(me % 2 == 0, y, x))
    for v in range(nv):
        _, spot = slot(v, 0, na)
        cols = []
        for half in range(2):
            r, l = right[half], left[half]
            wide = jnp.where(lane % 4 < 2, along(r, -spot - 2), along(l, 2 - spot))
            slim = jnp.where(lane % 4 < 2, along(r, -spot - 1), along(l, 1 - spot))
            cols.append(cols_ref[0, half_rows(half), :] * wide + cols_ref[1, half_rows(half), :] * slim)
        low, high = [], []
        for q in range(na // 4):
            rows = half_rows(v * (na // 4) + q)
            x, y = ahead_ref[rows, :], back_ref[rows, :]
            m, p = jnp.where(rad % 2 == 0, y, x), jnp.where(rad % 2 == 0, x, y)
            low.append(rows_ref[0, half_rows(q), :] * m + rows_ref[1, half_rows(q), :] * down(m, -1))
            high.append(rows_ref[2, half_rows(q), :] * p + rows_ref[3, half_rows(q), :] * down(p, 1))
        out.append((cols, low, high))
    return out


def spread(x, part, a, half, sub, lane):
    cols, low, high = part
    x = x + jnp.where((lane < 2) | (lane >= LANES - 2), along(cols[half], LANES - 2 - 4 * a), 0.0)
    j = a % 4
    if half == 0:
        return x + jnp.where(sub < 2, down(low[a // 4], -2 * j), 0.0)
    return x + jnp.where(sub >= SUB - 2, down(high[a // 4], SUB - 2 - 2 * j), 0.0)


def first_finish(routes, *refs):
    near_ref, jac_ref, src_ref, inv_ref, placed_ref, cols_ref, rows_ref = refs[:7]
    ahead_ref, back_ref, across_ref, *relayed = refs[7 : 10 + routes]
    direct = refs[10 + routes : 10 + 2 * routes]
    out_ref, rhs_ref, ahead_to, back_to, across_to, mate_to = refs[10 + 2 * routes :]
    nv, na = near_ref.shape[:2]
    sub, lane = iotas()
    share = shares(routes)
    mate_at = lambda half: relayed[SUB * half // share][SUB * half % share : SUB * half % share + SUB, :]
    parts = halo_sums(nv, na, ahead_ref, back_ref, across_ref, mate_at, cols_ref, rows_ref)
    me = lax.axis_index("circ")
    sources = [(ref, 0, donor_at(me - 2 * n)) for n, ref in enumerate(direct)]
    sources += [(ref, share, donor_at(me + 1 - 2 * (me % 2) - 2 * n)) for n, ref in enumerate(relayed)]
    packer = Packer(na, nv)
    for a in range(na):
        for half in range(2):
            rows = half_rows(half)
            near = [spread(near_ref[v, a, rows, :], parts[v], a, half, sub, lane) for v in range(nv)]
            inv = inv_ref[a, rows, :]
            for s in range(nv):
                acc = src_ref[s, a, rows, :]
                if a < 2:
                    acc = add_tiles(acc, sources, placed_ref, s, a, half, nv)
                rhs_ref[s, a, rows, :] = acc
                for b in range(nv):
                    acc = acc + jac_ref[s, b, a, rows, :] * near[b]
                x = acc * inv
                out_ref[s, a, rows, :] = x
                packer.add(s, a, half, x)
    packer.write(ahead_to, back_to, across_to, [mate_to.at[:SUB], mate_to.at[SUB:]])


def finish_kernel(last, *refs):
    base_ref, cols_ref, rows_ref, edge_cols, edge_low, edge_high = refs[:6]
    ahead_ref, back_ref, across_ref, mate_ref, out_ref, *rest = refs[6:]
    nv, na = base_ref.shape[:2]
    sub, lane = iotas()
    if last:
        result_ref, out_ref, sems = out_ref, *rest
        copies = []
    sums = halo_sums(
        nv, na, ahead_ref, back_ref, across_ref, lambda half: mate_ref[half_rows(half), :], cols_ref, rows_ref
    )
    parts = []
    for s in range(nv):
        turned = []
        for kind, edge_ref in enumerate((edge_cols, edge_low, edge_high)):
            turned.append([])
            for q in range(2 if kind == 0 else na // 4):
                total = edge_ref[s, 0, half_rows(q), :] * sums[0][kind][q]
                for b in range(1, nv):
                    total = total + edge_ref[s, b, half_rows(q), :] * sums[b][kind][q]
                turned[-1].append(total)
        parts.append(turned)
    packer = None if last else Packer(na, nv)
    for a in range(na):
        for half in range(2):
            for s in range(nv):
                x = spread(base_ref[s, a, half_rows(half), :], parts[s], a, half, sub, lane)
                out_ref[s, a, half_rows(half), :] = x
                if packer is not None:
                    packer.add(s, a, half, x)
        if last:
            copy = pltpu.make_async_copy(out_ref.at[:, a], result_ref.at[:, a], sems.at[a])
            copy.start()
            copies.append(copy)
    if last:
        for copy in copies:
            copy.wait()
    else:
        ahead_to, back_to, across_to, mate_to = rest
        packer.write(ahead_to, back_to, across_to, [mate_to.at[:SUB], mate_to.at[SUB:]])


def call(kernel, name, outs, args, specs=None, scratch=(), us=1, out_specs=None):
    vmem = pl.BlockSpec(memory_space=pltpu.VMEM)
    return pl.pallas_call(
        kernel,
        out_shape=outs,
        in_specs=[vmem] * len(args) if specs is None else specs,
        out_specs=[vmem] * len(outs) if out_specs is None else out_specs,
        scratch_shapes=list(scratch),
        compiler_params=PARAMS,
        cost_estimate=pl.CostEstimate(
            flops=us * 1_000_000, bytes_accessed=us * 3_000_000, transcendentals=0
        ),
        name=name,
    )(*args)


def solution(mesh):
    route = routes(mesh)
    vmem = lambda *shape: pltpu.VMEM(shape, jnp.float32)
    inside = pl.BlockSpec(memory_space=pltpu.VMEM)
    outside = pl.BlockSpec(memory_space=pltpu.HBM)
    far = lambda x: pltpu.with_memory_space_constraint(x, pltpu.HBM)

    def sent(x, pairs):
        return lax.ppermute(x, AXES, pairs)

    def per_device(adjoint, source, jacobian, couple, donor_row, target_row, tile_count, weights):
        nv, na, nr, nc = adjoint.shape[1:]
        donors, slots = donor_row.shape[2:]
        count = len(route["faces"])
        sides = 2 * nv * na
        edges = lambda across: [vmem(sides + SUB, nc), vmem(sides, nc), vmem(across, nc), vmem(nr, nc)]
        block = vmem(nv, na, nr, nc)
        lam, cpl, rhs, jac, placed, inv, edge_coefs, row_coefs, *tiles = call(
            load_kernel, "load",
            [block, vmem(12, na, nr, nc), block, vmem(nv, nv, na, nr, nc), vmem(donors, slots, nr, nc),
             vmem(na, nr, nc), vmem(2, nr, nc), vmem(4, 2 * na, nc)]
            + [vmem(4 * slots * nv + SUB * n, nc) for n in range(count)],
            [*map(far, (adjoint[0], donor_row[0], couple[0], source[0], jacobian[0], target_row[0],
                        tile_count[0], weights.reshape(-1, nc)))],
            [outside] * 8,
            [pltpu.SMEM(donor_row.shape[1:], jnp.int32), pltpu.SMEM(target_row.shape[1:], jnp.int32),
             pltpu.SMEM(tile_count.shape[1:], jnp.int32), pltpu.VMEM((donors * slots, nc), jnp.float32),
             pltpu.SemaphoreType.DMA((7 + nv,))],
        )
        ahead, back, cross, cols = call(pack_kernel, "pack", edges(sides - SUB), [lam])
        tiles = [sent(x, pairs) for x, pairs in zip(tiles, route["faces"])]
        for sweep in range(SWEEPS):
            last = sweep == SWEEPS - 1
            ahead = sent(ahead, route["ahead"])
            back = sent(back, route["back"])
            across = sent(cross, route["across"])
            if sweep == 0:
                share = shares(count)
                relayed = [
                    call(functools.partial(relay_kernel, share * n, share=share), f"relay{n}",
                         [vmem(share + 2 * slots * nv, nc)], [cols, x])[0]
                    for n, x in enumerate(tiles)
                ]
                relayed = [sent(x, route["mate"]) for x in relayed]
                near, = call(work_kernel, "work", [block], [lam, cpl])
                lam, rhs, ahead, back, cross, cols = call(
                    functools.partial(first_finish, count), "finish0", [block] * 2 + edges(nr + SUB),
                    [near, jac, rhs, inv, placed, edge_coefs, row_coefs, ahead, back, across,
                     *relayed, *tiles],
                )
                continue
            mate = sent(cols, route["mate"])
            prepare = sweep == 1
            base, *more = call(
                functools.partial(local_kernel, prepare), f"local{sweep}",
                [block] + ([vmem(nv, nv, nr, nc)] + [vmem(nv, nv, 2 * na, nc)] * 2 if prepare else []),
                [lam, cpl, jac, rhs, inv],
            )
            if prepare:
                matrices = more
            scratch, spaces, outs = [], None, [block] + edges(nr + SUB)
            if last:
                outs, spaces = [jax.ShapeDtypeStruct((nv, na, nr, nc), jnp.float32)], [outside]
                scratch = [pltpu.VMEM((nv, na, nr, nc), jnp.float32), pltpu.SemaphoreType.DMA((na,))]
            lam, *more = call(
                functools.partial(finish_kernel, last), f"finish{sweep}", outs,
                [base, edge_coefs, row_coefs, *matrices, ahead, back, across, mate], None, scratch, 1, spaces,
            )
            if not last:
                ahead, back, cross, cols = more
        return lam[None]

    in_specs = (
        P("sec", None, None, "rad", "circ"),
        P("sec", None, None, "rad", "circ"),
        P("sec", None, None, None, "rad", "circ"),
        P("sec", None, None, "rad", "circ"),
        P("rad", None, None, None),
        P("rad", None, None, None),
        P("rad", None, None),
        P("rad", None, "circ", None, None),
    )
    out_specs = P("sec", None, None, "rad", "circ")
    return jax.shard_map(
        per_device, mesh=mesh, in_specs=in_specs, out_specs=out_specs, check_vma=False
    )
```

```python
import functools

import jax
import jax.numpy as jnp
from jax import lax
from jax.experimental import pallas as pl
from jax.experimental.pallas import tpu as pltpu
from jax.sharding import PartitionSpec as P

SWEEPS = 3
AXES = ("sec", "circ", "rad")
SUB, LANES = 8, 128
PARAMS = pltpu.CompilerParams(vmem_limit_bytes=16 * 1024 * 1024)


def routes(mesh):
    secs, circs, rads = (mesh.shape[a] for a in AXES)

    def pairs(target):
        flat = lambda s, c, r: (s * circs + c) * rads + r
        return [
            (flat(s, c, r), flat(*target(s, c, r)))
            for s in range(secs)
            for c in range(circs)
            for r in range(rads)
        ]

    def swap(s, c, r, odd):
        q = r + 1 if (r + odd) % 2 == 0 else r - 1
        return (s, c, q) if 0 <= q < rads else (s, c ^ 1, r)

    return {
        "ahead": pairs(lambda s, c, r: swap(s, c, r, 0)),
        "back": pairs(lambda s, c, r: swap(s, c, r, 1)),
        "mate": pairs(lambda s, c, r: (s, c ^ 1, r)),
        "across": pairs(lambda s, c, r: (s, (c - 1 if c % 2 == 0 else c + 1) % circs, r)),
        "faces": [
            pairs(lambda s, c, r: (1, (c + k) % circs, r) if s == 0 else (0, (c - k) % circs, r))
            for k in range(0, circs, 2)
        ],
    }


def iotas():
    sub = lax.broadcasted_iota(jnp.int32, (SUB, LANES), 0)
    lane = lax.broadcasted_iota(jnp.int32, (SUB, LANES), 1)
    return sub, lane


def down(x, by):
    return pltpu.roll(x, by % SUB, 0) if by % SUB else x


def along(x, by):
    return pltpu.roll(x, by % LANES, 1) if by % LANES else x


def half_rows(half):
    return slice(SUB * half, SUB * (half + 1))


def slot(v, a, na):
    return v % 2, 4 * (na * (v // 2) + a) + 2 * (v % 2)


class Packer:
    def __init__(self, na, nv):
        self.sub, self.lane = iotas()
        self.na = na
        self.low, self.high, self.cols = {}, {}, {}

    def put(self, book, key, keep, x):
        book[key] = jnp.where(keep, x, book[key]) if key in book else x

    def add(self, v, a, half, x):
        k = v * self.na + a
        group, j = k // 4, k % 4
        inside = (self.sub >= 2 * j) & (self.sub < 2 * j + 2)
        if half == 0:
            self.put(self.low, group, inside, down(x, 2 * j))
        else:
            self.put(self.high, group, inside, down(x, 2 * j + 2))
        part, spot = slot(v, a, self.na)
        inside = (self.lane >= spot) & (self.lane < spot + 4)
        self.put(self.cols, (part, half), inside, along(x, spot + 2))

    def write(self, ahead_ref, back_ref, across_ref, mate_refs):
        even = lax.axis_index("rad") % 2 == 0
        for g in range(len(self.low)):
            rows = slice(SUB * g, SUB * (g + 1))
            ahead_ref[rows, :] = jnp.where(even, self.high[g], self.low[g])
            back_ref[rows, :] = jnp.where(even, self.low[g], self.high[g])
        even = lax.axis_index("circ") % 2 == 0
        for half in range(2):
            x, y = self.cols[0, half], self.cols[1, half]
            right = jnp.where(self.lane % 4 < 2, x, y)
            left = jnp.where(self.lane % 4 < 2, y, x)
            rows = slice(SUB * half, SUB * (half + 1))
            across_ref[rows, :] = jnp.where(even, left, right)
            mate_refs[half][...] = jnp.where(even, right, left)


def pack_kernel(lam_ref, ahead_ref, back_ref, across_ref, mate_ref):
    nv, na = lam_ref.shape[:2]
    packer = Packer(na, nv)
    for a in range(na):
        for v in range(nv):
            for half in range(2):
                packer.add(v, a, half, lam_ref[v, a, SUB * half : SUB * (half + 1), :])
    packer.write(ahead_ref, back_ref, across_ref, [mate_ref.at[:SUB], mate_ref.at[SUB:]])


def fetch_kernel(couple_ref, jac_in, targets_in, counts_in, weights_in, *refs):
    jac_ref, placed_ref, inv_ref, cols_ref, rows_ref, targets_ref, counts_ref, weights_ref, sems = refs
    count = jac_ref.shape[0]
    slim = [
        pltpu.make_async_copy(targets_in, targets_ref, sems.at[count]),
        pltpu.make_async_copy(counts_in, counts_ref, sems.at[count + 1]),
        pltpu.make_async_copy(weights_in, weights_ref, sems.at[count + 2]),
    ]
    wide = [pltpu.make_async_copy(jac_in.at[s], jac_ref.at[s], sems.at[s]) for s in range(count)]
    for copy in slim + wide:
        copy.start()
    coefs_of(couple_ref, inv_ref, cols_ref, rows_ref)
    for copy in slim:
        copy.wait()
    place_weights(targets_ref, counts_ref, weights_ref, placed_ref)
    for copy in wide:
        copy.wait()


def load_kernel(adjoint_ref, donors_in, couple_in, src_in, *refs):
    lam_ref, couple_ref, src_ref, *tile_refs, donors_ref, sems = refs
    nv, na, nr, _ = lam_ref.shape
    copies = [
        pltpu.make_async_copy(donors_in, donors_ref, sems.at[0]),
        pltpu.make_async_copy(adjoint_ref, lam_ref, sems.at[1]),
        pltpu.make_async_copy(couple_in, couple_ref, sems.at[2]),
        pltpu.make_async_copy(src_in, src_ref, sems.at[3]),
    ]
    for copy in copies:
        copy.start()
    copies[0].wait()
    copies[1].wait()
    me, circs, slots = lax.axis_index("circ"), donors_ref.shape[1], donors_ref.shape[2]
    for n, tile_ref in enumerate(tile_refs):
        reader = jnp.where(me + 2 * n >= circs, me + 2 * n - circs, me + 2 * n)
        for part, to in enumerate((reader, reader + 1 - 2 * (reader % 2))):
            for k in range(slots):
                row = jnp.clip(donors_ref[me, to, k], 0, nr - 1)
                for v in range(nv):
                    for a in range(2):
                        at = ((part * slots + k) * nv + v) * 2 + a
                        tile_ref[at : at + 1, :] = lam_ref[v, na - 2 + a, pl.ds(row, 1), :]
    for copy in copies[2:]:
        copy.wait()


def place_weights(targets_ref, counts_ref, weights_ref, placed_ref):
    me = lax.axis_index("circ")
    stator = lax.axis_index("sec") == 1
    sub, _ = iotas()
    slots = targets_ref.shape[-1]
    for d in range(targets_ref.shape[0]):
        for k in range(slots):
            live = (k < counts_ref[d, me]) & stator
            row = jnp.where(live, targets_ref[d, me, k], -1)
            w = jnp.broadcast_to(weights_ref[d * slots + k : d * slots + k + 1, :], (SUB, LANES))
            for h in range(2):
                placed_ref[d, k, SUB * h : SUB * (h + 1), :] = jnp.where(sub + SUB * h == row, w, 0.0)


def inner_coefs(c, half, sub, lane):
    c = list(c)
    if half == 0:
        c[4] = jnp.where(sub >= 2, c[4], 0.0)
        c[5] = jnp.where(sub >= 1, c[5], 0.0)
    else:
        c[6] = jnp.where(sub < SUB - 1, c[6], 0.0)
        c[7] = jnp.where(sub < SUB - 2, c[7], 0.0)
    c[8] = jnp.where(lane >= 2, c[8], 0.0)
    c[9] = jnp.where(lane >= 1, c[9], 0.0)
    c[10] = jnp.where(lane < LANES - 1, c[10], 0.0)
    c[11] = jnp.where(lane < LANES - 2, c[11], 0.0)
    return c


def local_sums(lam_ref, a, coef, sub):
    nv, na = lam_ref.shape[:2]
    sums = []
    for v in range(nv):
        x = [lam_ref[v, a, half_rows(h), :] for h in range(2)]
        moved = {o: [down(x[h], -o) for h in range(2)] for o in (-2, -1, 1, 2)}
        both = []
        for half in range(2):
            c = coef[half]
            total = None
            for i, o in enumerate((-2, -1, 1, 2)):
                if 0 <= a + o < na:
                    term = c[i] * lam_ref[v, a + o, half_rows(half), :]
                    total = term if total is None else total + term
            for i, o in enumerate((-2, -1, 1, 2)):
                m = moved[o]
                if o < 0:
                    y = m[0] if half == 0 else jnp.where(sub >= -o, m[1], m[0])
                else:
                    y = m[1] if half == 1 else jnp.where(sub < SUB - o, m[0], m[1])
                total = total + c[4 + i] * y
            for i, o in enumerate((-2, -1, 1, 2)):
                total = total + c[8 + i] * along(x[half], -o)
            both.append(total)
        sums.append(both)
    return sums


class Gather:
    def __init__(self, sub, lane):
        self.sub, self.lane = sub, lane
        self.got = {}

    def put(self, key, keep, x):
        self.got[key] = jnp.where(keep, x, self.got[key]) if key in self.got else x

    def cols(self, name, half, a, x):
        inside = (self.lane >= 4 * a) & (self.lane < 4 * a + 4)
        self.put((name, half), inside, along(x, 4 * a + 2))

    def rows(self, name, half, a, x):
        j = a % 4
        inside = (self.sub >= 2 * j) & (self.sub < 2 * j + 2)
        self.put((name, a // 4), inside, down(x, 2 * j + 2 * half))


def coefs_of(couple_ref, inv_ref, cols_ref, rows_ref):
    na = couple_ref.shape[1]
    sub, lane = iotas()
    rad = lax.axis_index("rad")
    has_low, has_high = rad > 0, rad < lax.axis_size("rad") - 1
    gather = Gather(sub, lane)
    for a in range(na):
        for half in range(2):
            c = [couple_ref[i, a, half_rows(half), :] for i in range(12)]
            total = c[0]
            for i in range(1, 12):
                total = total + c[i]
            inv_ref[a, half_rows(half), :] = 1.0 / (1.0 + total)
            gather.cols("outer", half, a, jnp.where(lane < 2, c[8], jnp.where(lane >= LANES - 2, c[11], 0.0)))
            gather.cols("inner", half, a, jnp.where(lane < 1, c[9], jnp.where(lane >= LANES - 1, c[10], 0.0)))
            if half == 0:
                gather.rows("low far", 0, a, jnp.where(has_low, c[4], 0.0))
                gather.rows("low nigh", 0, a, jnp.where(has_low & (sub < 1), c[5], 0.0))
            else:
                gather.rows("high far", 1, a, jnp.where(has_high, c[7], 0.0))
                gather.rows("high nigh", 1, a, jnp.where(has_high & (sub >= SUB - 1), c[6], 0.0))
    for i, name in enumerate(("outer", "inner")):
        for half in range(2):
            cols_ref[i, half_rows(half), :] = gather.got[name, half]
    for i, name in enumerate(("low far", "low nigh", "high far", "high nigh")):
        for q in range(na // 4):
            rows_ref[i, half_rows(q), :] = gather.got[name, q]


def work_kernel(lam_ref, couple_ref, near_ref):
    sub, lane = iotas()
    for a in range(lam_ref.shape[1]):
        coef = [
            inner_coefs([couple_ref[i, a, half_rows(h), :] for i in range(12)], h, sub, lane) for h in range(2)
        ]
        for v, both in enumerate(local_sums(lam_ref, a, coef, sub)):
            for half, x in enumerate(both):
                near_ref[v, a, half_rows(half), :] = x


def donor_at(at):
    return jnp.where(at < 0, at + lax.axis_size("circ"), at)


def add_tiles(x, sources, placed_ref, s, a, half, nv):
    for tile_ref, start, donor in sources:
        for t in range(placed_ref.shape[1]):
            at = start + (t * nv + s) * 2 + a
            tile = jnp.broadcast_to(tile_ref[at : at + 1, :], (SUB, LANES))
            x = x + placed_ref[donor, t, half_rows(half), :] * tile
    return x


def local_kernel(prepare, lam_ref, couple_ref, jac_ref, rhs_ref, inv_ref, base_ref, *edge_refs):
    nv, na = lam_ref.shape[:2]
    sub, lane = iotas()
    gathers = {}
    for a in range(na):
        coef = [
            inner_coefs([couple_ref[i, a, half_rows(h), :] for i in range(12)], h, sub, lane) for h in range(2)
        ]
        near = local_sums(lam_ref, a, coef, sub)
        for half in range(2):
            inv = inv_ref[a, half_rows(half), :]
            for s in range(nv):
                acc = rhs_ref[s, a, half_rows(half), :]
                for b in range(nv):
                    m = jac_ref[s, b, a, half_rows(half), :]
                    acc = acc + m * near[b][half]
                    if prepare:
                        m = m * inv
                        gather = gathers.setdefault((s, b), Gather(sub, lane))
                        gather.cols("cols", half, a, m)
                        gather.rows("high" if half else "low", half, a, m)
                base_ref[s, a, half_rows(half), :] = acc * inv
    if prepare:
        cols_ref, low_ref, high_ref = edge_refs
        for (s, b), gather in gathers.items():
            for half in range(2):
                cols_ref[s, b, half_rows(half), :] = gather.got["cols", half]
            for q in range(na // 4):
                low_ref[s, b, half_rows(q), :] = gather.got["low", q]
                high_ref[s, b, half_rows(q), :] = gather.got["high", q]


def relay_kernel(first, cols_ref, tile_ref, _, out_ref, *, share):
    half = out_ref.shape[0] - share
    out_ref[share:, :] = tile_ref[half : 2 * half, :]
    if first < cols_ref.shape[0]:
        out_ref[:share, :] = cols_ref[first : first + share, :]


def shares(routes):
    return SUB * max(1, 2 // routes)


def halo_sums(nv, na, ahead_ref, back_ref, across_ref, mate_at, cols_ref, rows_ref):
    sub, lane = iotas()
    me, rad = lax.axis_index("circ"), lax.axis_index("rad")
    out = []
    right, left = [], []
    for half in range(2):
        x, y = mate_at(half), across_ref[half_rows(half), :]
        right.append(jnp.where(me % 2 == 0, x, y))
        left.append(jnp.where(me % 2 == 0, y, x))
    for v in range(nv):
        _, spot = slot(v, 0, na)
        cols = []
        for half in range(2):
            r, l = right[half], left[half]
            wide = jnp.where(lane % 4 < 2, along(r, -spot - 2), along(l, 2 - spot))
            slim = jnp.where(lane % 4 < 2, along(r, -spot - 1), along(l, 1 - spot))
            cols.append(cols_ref[0, half_rows(half), :] * wide + cols_ref[1, half_rows(half), :] * slim)
        low, high = [], []
        for q in range(na // 4):
            rows = half_rows(v * (na // 4) + q)
            x, y = ahead_ref[rows, :], back_ref[rows, :]
            m, p = jnp.where(rad % 2 == 0, y, x), jnp.where(rad % 2 == 0, x, y)
            low.append(rows_ref[0, half_rows(q), :] * m + rows_ref[1, half_rows(q), :] * down(m, -1))
            high.append(rows_ref[2, half_rows(q), :] * p + rows_ref[3, half_rows(q), :] * down(p, 1))
        out.append((cols, low, high))
    return out


def spread(x, part, a, half, sub, lane):
    cols, low, high = part
    x = x + jnp.where((lane < 2) | (lane >= LANES - 2), along(cols[half], LANES - 2 - 4 * a), 0.0)
    j = a % 4
    if half == 0:
        return x + jnp.where(sub < 2, down(low[a // 4], -2 * j), 0.0)
    return x + jnp.where(sub >= SUB - 2, down(high[a // 4], SUB - 2 - 2 * j), 0.0)


def first_finish(routes, *refs):
    near_ref, jac_ref, src_ref, inv_ref, placed_ref, cols_ref, rows_ref = refs[:7]
    ahead_ref, back_ref, across_ref, *relayed = refs[7 : 10 + routes]
    direct = refs[10 + routes : 10 + 2 * routes]
    out_ref, rhs_ref, ahead_to, back_to, across_to, mate_to = refs[10 + 2 * routes :]
    nv, na = near_ref.shape[:2]
    sub, lane = iotas()
    share = shares(routes)
    mate_at = lambda half: relayed[SUB * half // share][SUB * half % share : SUB * half % share + SUB, :]
    parts = halo_sums(nv, na, ahead_ref, back_ref, across_ref, mate_at, cols_ref, rows_ref)
    me = lax.axis_index("circ")
    sources = [(ref, 0, donor_at(me - 2 * n)) for n, ref in enumerate(direct)]
    sources += [(ref, share, donor_at(me + 1 - 2 * (me % 2) - 2 * n)) for n, ref in enumerate(relayed)]
    packer = Packer(na, nv)
    for a in range(na):
        for half in range(2):
            rows = half_rows(half)
            near = [spread(near_ref[v, a, rows, :], parts[v], a, half, sub, lane) for v in range(nv)]
            inv = inv_ref[a, rows, :]
            for s in range(nv):
                acc = src_ref[s, a, rows, :]
                if a < 2:
                    acc = add_tiles(acc, sources, placed_ref, s, a, half, nv)
                rhs_ref[s, a, rows, :] = acc
                for b in range(nv):
                    acc = acc + jac_ref[s, b, a, rows, :] * near[b]
                x = acc * inv
                out_ref[s, a, rows, :] = x
                packer.add(s, a, half, x)
    packer.write(ahead_to, back_to, across_to, [mate_to.at[:SUB], mate_to.at[SUB:]])


def finish_kernel(last, *refs):
    base_ref, cols_ref, rows_ref, edge_cols, edge_low, edge_high = refs[:6]
    ahead_ref, back_ref, across_ref, mate_ref, out_ref, *rest = refs[6:]
    nv, na = base_ref.shape[:2]
    sub, lane = iotas()
    if last:
        result_ref, out_ref, sems = out_ref, *rest
        copies = []
    sums = halo_sums(
        nv, na, ahead_ref, back_ref, across_ref, lambda half: mate_ref[half_rows(half), :], cols_ref, rows_ref
    )
    parts = []
    for s in range(nv):
        turned = []
        for kind, edge_ref in enumerate((edge_cols, edge_low, edge_high)):
            turned.append([])
            for q in range(2 if kind == 0 else na // 4):
                total = edge_ref[s, 0, half_rows(q), :] * sums[0][kind][q]
                for b in range(1, nv):
                    total = total + edge_ref[s, b, half_rows(q), :] * sums[b][kind][q]
                turned[-1].append(total)
        parts.append(turned)
    packer = None if last else Packer(na, nv)
    for a in range(na):
        for half in range(2):
            for s in range(nv):
                x = spread(base_ref[s, a, half_rows(half), :], parts[s], a, half, sub, lane)
                out_ref[s, a, half_rows(half), :] = x
                if packer is not None:
                    packer.add(s, a, half, x)
        if last:
            copy = pltpu.make_async_copy(out_ref.at[:, a], result_ref.at[:, a], sems.at[a])
            copy.start()
            copies.append(copy)
    if last:
        for copy in copies:
            copy.wait()
    else:
        ahead_to, back_to, across_to, mate_to = rest
        packer.write(ahead_to, back_to, across_to, [mate_to.at[:SUB], mate_to.at[SUB:]])


def call(kernel, name, outs, args, specs=None, scratch=(), us=1, out_specs=None):
    vmem = pl.BlockSpec(memory_space=pltpu.VMEM)
    return pl.pallas_call(
        kernel,
        out_shape=outs,
        in_specs=[vmem] * len(args) if specs is None else specs,
        out_specs=[vmem] * len(outs) if out_specs is None else out_specs,
        scratch_shapes=list(scratch),
        compiler_params=PARAMS,
        cost_estimate=pl.CostEstimate(
            flops=us * 1_000_000, bytes_accessed=us * 3_000_000, transcendentals=0
        ),
        name=name,
    )(*args)


def solution(mesh):
    route = routes(mesh)
    vmem = lambda *shape: pltpu.VMEM(shape, jnp.float32)
    inside = pl.BlockSpec(memory_space=pltpu.VMEM)
    outside = pl.BlockSpec(memory_space=pltpu.HBM)
    unread = pl.BlockSpec(memory_space=pl.ANY)
    far = lambda x: pltpu.with_memory_space_constraint(x, pltpu.HBM)

    def sent(x, pairs):
        return lax.ppermute(x, AXES, pairs)

    def per_device(adjoint, source, jacobian, couple, donor_row, target_row, tile_count, weights):
        nv, na, nr, nc = adjoint.shape[1:]
        donors, slots = donor_row.shape[2:]
        count = len(route["faces"])
        sides = 2 * nv * na
        edges = lambda across: [vmem(sides + SUB, nc), vmem(sides, nc), vmem(across, nc), vmem(nr, nc)]
        block = vmem(nv, na, nr, nc)
        lam, cpl, rhs, *tiles = call(
            load_kernel, "load",
            [block, vmem(12, na, nr, nc), block] + [vmem(4 * slots * nv + SUB * n, nc) for n in range(count)],
            [*map(far, (adjoint[0], donor_row[0], couple[0], source[0]))], [outside] * 4,
            [pltpu.SMEM(donor_row.shape[1:], jnp.int32), pltpu.SemaphoreType.DMA((4,))],
        )
        ahead, back, cross, cols = call(pack_kernel, "pack", edges(sides - SUB), [lam])
        tiles = [sent(x, pairs) for x, pairs in zip(tiles, route["faces"])]
        for sweep in range(SWEEPS):
            last = sweep == SWEEPS - 1
            ahead = sent(ahead, route["ahead"])
            back = sent(back, route["back"])
            across = sent(cross, route["across"])
            if sweep == 0:
                share = shares(count)
                jac, placed, inv, edge_coefs, row_coefs = call(
                    fetch_kernel, "fetch",
                    [vmem(nv, nv, na, nr, nc), vmem(donors, slots, nr, nc), vmem(na, nr, nc),
                     vmem(2, nr, nc), vmem(4, 2 * na, nc)],
                    [cpl, *map(far, (jacobian[0], target_row[0], tile_count[0], weights.reshape(-1, nc)))],
                    [inside] + [outside] * 4,
                    [pltpu.SMEM(target_row.shape[1:], jnp.int32), pltpu.SMEM(tile_count.shape[1:], jnp.int32),
                     pltpu.VMEM((donors * slots, nc), jnp.float32), pltpu.SemaphoreType.DMA((nv + 3,))],
                )
                relayed = [
                    call(functools.partial(relay_kernel, share * n, share=share), f"relay{n}",
                         [vmem(share + 2 * slots * nv, nc)], [cols, x, inv], [inside] * 2 + [unread])[0]
                    for n, x in enumerate(tiles)
                ]
                relayed = [sent(x, route["mate"]) for x in relayed]
                near, = call(work_kernel, "work", [block], [lam, cpl])
                lam, rhs, ahead, back, cross, cols = call(
                    functools.partial(first_finish, count), "finish0", [block] * 2 + edges(nr + SUB),
                    [near, jac, rhs, inv, placed, edge_coefs, row_coefs, ahead, back, across,
                     *relayed, *tiles],
                )
                continue
            mate = sent(cols, route["mate"])
            prepare = sweep == 1
            base, *more = call(
                functools.partial(local_kernel, prepare), f"local{sweep}",
                [block] + ([vmem(nv, nv, nr, nc)] + [vmem(nv, nv, 2 * na, nc)] * 2 if prepare else []),
                [lam, cpl, jac, rhs, inv],
            )
            if prepare:
                matrices = more
            scratch, spaces, outs = [], None, [block] + edges(nr + SUB)
            if last:
                outs, spaces = [jax.ShapeDtypeStruct((nv, na, nr, nc), jnp.float32)], [outside]
                scratch = [pltpu.VMEM((nv, na, nr, nc), jnp.float32), pltpu.SemaphoreType.DMA((na,))]
            lam, *more = call(
                functools.partial(finish_kernel, last), f"finish{sweep}", outs,
                [base, edge_coefs, row_coefs, *matrices, ahead, back, across, mate], None, scratch, 1, spaces,
            )
            if not last:
                ahead, back, cross, cols = more
        return lam[None]

    in_specs = (
        P("sec", None, None, "rad", "circ"),
        P("sec", None, None, "rad", "circ"),
        P("sec", None, None, None, "rad", "circ"),
        P("sec", None, None, "rad", "circ"),
        P("rad", None, None, None),
        P("rad", None, None, None),
        P("rad", None, None),
        P("rad", None, "circ", None, None),
    )
    out_specs = P("sec", None, None, "rad", "circ")
    return jax.shard_map(
        per_device, mesh=mesh, in_specs=in_specs, out_specs=out_specs, check_vma=False
    )
```

```python
import functools

import jax
import jax.numpy as jnp
from jax import lax
from jax.experimental import pallas as pl
from jax.experimental.pallas import tpu as pltpu
from jax.sharding import PartitionSpec as P

SWEEPS = 3
AXES = ("sec", "circ", "rad")
SUB, LANES = 8, 128
PARAMS = pltpu.CompilerParams(vmem_limit_bytes=16 * 1024 * 1024)


def routes(mesh):
    secs, circs, rads = (mesh.shape[a] for a in AXES)

    def pairs(target):
        flat = lambda s, c, r: (s * circs + c) * rads + r
        return [
            (flat(s, c, r), flat(*target(s, c, r)))
            for s in range(secs)
            for c in range(circs)
            for r in range(rads)
        ]

    def swap(s, c, r, odd):
        q = r + 1 if (r + odd) % 2 == 0 else r - 1
        return (s, c, q) if 0 <= q < rads else (s, c ^ 1, r)

    return {
        "ahead": pairs(lambda s, c, r: swap(s, c, r, 0)),
        "back": pairs(lambda s, c, r: swap(s, c, r, 1)),
        "mate": pairs(lambda s, c, r: (s, c ^ 1, r)),
        "across": pairs(lambda s, c, r: (s, (c - 1 if c % 2 == 0 else c + 1) % circs, r)),
        "faces": [
            pairs(lambda s, c, r: (1, (c + k) % circs, r) if s == 0 else (0, (c - k) % circs, r))
            for k in range(0, circs, 2)
        ],
    }


def iotas():
    sub = lax.broadcasted_iota(jnp.int32, (SUB, LANES), 0)
    lane = lax.broadcasted_iota(jnp.int32, (SUB, LANES), 1)
    return sub, lane


def down(x, by):
    return pltpu.roll(x, by % SUB, 0) if by % SUB else x


def along(x, by):
    return pltpu.roll(x, by % LANES, 1) if by % LANES else x


def half_rows(half):
    return slice(SUB * half, SUB * (half + 1))


def slot(v, a, na):
    return v % 2, 4 * (na * (v // 2) + a) + 2 * (v % 2)


class Packer:
    def __init__(self, na, nv):
        self.sub, self.lane = iotas()
        self.na = na
        self.low, self.high, self.cols = {}, {}, {}

    def put(self, book, key, keep, x):
        book[key] = jnp.where(keep, x, book[key]) if key in book else x

    def add(self, v, a, half, x):
        k = v * self.na + a
        group, j = k // 4, k % 4
        inside = (self.sub >= 2 * j) & (self.sub < 2 * j + 2)
        if half == 0:
            self.put(self.low, group, inside, down(x, 2 * j))
        else:
            self.put(self.high, group, inside, down(x, 2 * j + 2))
        part, spot = slot(v, a, self.na)
        inside = (self.lane >= spot) & (self.lane < spot + 4)
        self.put(self.cols, (part, half), inside, along(x, spot + 2))

    def write(self, ahead_ref, back_ref, across_ref, mate_refs):
        even = lax.axis_index("rad") % 2 == 0
        for g in range(len(self.low)):
            rows = slice(SUB * g, SUB * (g + 1))
            ahead_ref[rows, :] = jnp.where(even, self.high[g], self.low[g])
            back_ref[rows, :] = jnp.where(even, self.low[g], self.high[g])
        even = lax.axis_index("circ") % 2 == 0
        for half in range(2):
            x, y = self.cols[0, half], self.cols[1, half]
            right = jnp.where(self.lane % 4 < 2, x, y)
            left = jnp.where(self.lane % 4 < 2, y, x)
            rows = slice(SUB * half, SUB * (half + 1))
            across_ref[rows, :] = jnp.where(even, left, right)
            mate_refs[half][...] = jnp.where(even, right, left)


def pack_kernel(lam_ref, ahead_ref, back_ref, across_ref, mate_ref):
    nv, na = lam_ref.shape[:2]
    packer = Packer(na, nv)
    for a in range(na):
        for v in range(nv):
            for half in range(2):
                packer.add(v, a, half, lam_ref[v, a, SUB * half : SUB * (half + 1), :])
    packer.write(ahead_ref, back_ref, across_ref, [mate_ref.at[:SUB], mate_ref.at[SUB:]])


def fetch_kernel(couple_ref, jac_in, targets_in, counts_in, weights_in, *refs):
    jac_ref, placed_ref, inv_ref, cols_ref, rows_ref, *edge_refs = refs[:8]
    targets_ref, counts_ref, weights_ref, sems = refs[8:]
    count = jac_ref.shape[0]
    slim = [
        pltpu.make_async_copy(targets_in, targets_ref, sems.at[count]),
        pltpu.make_async_copy(counts_in, counts_ref, sems.at[count + 1]),
        pltpu.make_async_copy(weights_in, weights_ref, sems.at[count + 2]),
    ]
    wide = [pltpu.make_async_copy(jac_in.at[s], jac_ref.at[s], sems.at[s]) for s in range(count)]
    for copy in slim + wide:
        copy.start()
    coefs_of(couple_ref, inv_ref, cols_ref, rows_ref)
    for copy in slim:
        copy.wait()
    place_weights(targets_ref, counts_ref, weights_ref, placed_ref)
    for s, copy in enumerate(wide):
        copy.wait()
        edge_matrices(s, jac_ref, inv_ref, *edge_refs)


def edge_matrices(s, jac_ref, inv_ref, cols_ref, low_ref, high_ref):
    nv, na = jac_ref.shape[1:3]
    sub, lane = iotas()
    for b in range(nv):
        gather = Gather(sub, lane)
        for a in range(na):
            for half in range(2):
                m = jac_ref[s, b, a, half_rows(half), :] * inv_ref[a, half_rows(half), :]
                gather.cols("cols", half, a, m)
                gather.rows("high" if half else "low", half, a, m)
        for half in range(2):
            cols_ref[s, b, half_rows(half), :] = gather.got["cols", half]
        for q in range(na // 4):
            low_ref[s, b, half_rows(q), :] = gather.got["low", q]
            high_ref[s, b, half_rows(q), :] = gather.got["high", q]


def load_kernel(adjoint_ref, donors_in, couple_in, src_in, *refs):
    lam_ref, couple_ref, src_ref, *tile_refs, donors_ref, sems = refs
    nv, na, nr, _ = lam_ref.shape
    copies = [
        pltpu.make_async_copy(donors_in, donors_ref, sems.at[0]),
        pltpu.make_async_copy(adjoint_ref, lam_ref, sems.at[1]),
        pltpu.make_async_copy(couple_in, couple_ref, sems.at[2]),
        pltpu.make_async_copy(src_in, src_ref, sems.at[3]),
    ]
    for copy in copies:
        copy.start()
    copies[0].wait()
    copies[1].wait()
    me, circs, slots = lax.axis_index("circ"), donors_ref.shape[1], donors_ref.shape[2]
    for n, tile_ref in enumerate(tile_refs):
        reader = jnp.where(me + 2 * n >= circs, me + 2 * n - circs, me + 2 * n)
        for part, to in enumerate((reader, reader + 1 - 2 * (reader % 2))):
            for k in range(slots):
                row = jnp.clip(donors_ref[me, to, k], 0, nr - 1)
                for v in range(nv):
                    for a in range(2):
                        at = ((part * slots + k) * nv + v) * 2 + a
                        tile_ref[at : at + 1, :] = lam_ref[v, na - 2 + a, pl.ds(row, 1), :]
    for copy in copies[2:]:
        copy.wait()


def place_weights(targets_ref, counts_ref, weights_ref, placed_ref):
    me = lax.axis_index("circ")
    stator = lax.axis_index("sec") == 1
    sub, _ = iotas()
    slots = targets_ref.shape[-1]
    for d in range(targets_ref.shape[0]):
        for k in range(slots):
            live = (k < counts_ref[d, me]) & stator
            row = jnp.where(live, targets_ref[d, me, k], -1)
            w = jnp.broadcast_to(weights_ref[d * slots + k : d * slots + k + 1, :], (SUB, LANES))
            for h in range(2):
                placed_ref[d, k, SUB * h : SUB * (h + 1), :] = jnp.where(sub + SUB * h == row, w, 0.0)


def inner_coefs(c, half, sub, lane):
    c = list(c)
    if half == 0:
        c[4] = jnp.where(sub >= 2, c[4], 0.0)
        c[5] = jnp.where(sub >= 1, c[5], 0.0)
    else:
        c[6] = jnp.where(sub < SUB - 1, c[6], 0.0)
        c[7] = jnp.where(sub < SUB - 2, c[7], 0.0)
    c[8] = jnp.where(lane >= 2, c[8], 0.0)
    c[9] = jnp.where(lane >= 1, c[9], 0.0)
    c[10] = jnp.where(lane < LANES - 1, c[10], 0.0)
    c[11] = jnp.where(lane < LANES - 2, c[11], 0.0)
    return c


def local_sums(lam_ref, a, coef, sub):
    nv, na = lam_ref.shape[:2]
    sums = []
    for v in range(nv):
        x = [lam_ref[v, a, half_rows(h), :] for h in range(2)]
        moved = {o: [down(x[h], -o) for h in range(2)] for o in (-2, -1, 1, 2)}
        both = []
        for half in range(2):
            c = coef[half]
            total = None
            for i, o in enumerate((-2, -1, 1, 2)):
                if 0 <= a + o < na:
                    term = c[i] * lam_ref[v, a + o, half_rows(half), :]
                    total = term if total is None else total + term
            for i, o in enumerate((-2, -1, 1, 2)):
                m = moved[o]
                if o < 0:
                    y = m[0] if half == 0 else jnp.where(sub >= -o, m[1], m[0])
                else:
                    y = m[1] if half == 1 else jnp.where(sub < SUB - o, m[0], m[1])
                total = total + c[4 + i] * y
            for i, o in enumerate((-2, -1, 1, 2)):
                total = total + c[8 + i] * along(x[half], -o)
            both.append(total)
        sums.append(both)
    return sums


class Gather:
    def __init__(self, sub, lane):
        self.sub, self.lane = sub, lane
        self.got = {}

    def put(self, key, keep, x):
        self.got[key] = jnp.where(keep, x, self.got[key]) if key in self.got else x

    def cols(self, name, half, a, x):
        inside = (self.lane >= 4 * a) & (self.lane < 4 * a + 4)
        self.put((name, half), inside, along(x, 4 * a + 2))

    def rows(self, name, half, a, x):
        j = a % 4
        inside = (self.sub >= 2 * j) & (self.sub < 2 * j + 2)
        self.put((name, a // 4), inside, down(x, 2 * j + 2 * half))


def coefs_of(couple_ref, inv_ref, cols_ref, rows_ref):
    na = couple_ref.shape[1]
    sub, lane = iotas()
    rad = lax.axis_index("rad")
    has_low, has_high = rad > 0, rad < lax.axis_size("rad") - 1
    gather = Gather(sub, lane)
    for a in range(na):
        for half in range(2):
            c = [couple_ref[i, a, half_rows(half), :] for i in range(12)]
            total = c[0]
            for i in range(1, 12):
                total = total + c[i]
            inv_ref[a, half_rows(half), :] = 1.0 / (1.0 + total)
            gather.cols("outer", half, a, jnp.where(lane < 2, c[8], jnp.where(lane >= LANES - 2, c[11], 0.0)))
            gather.cols("inner", half, a, jnp.where(lane < 1, c[9], jnp.where(lane >= LANES - 1, c[10], 0.0)))
            if half == 0:
                gather.rows("low far", 0, a, jnp.where(has_low, c[4], 0.0))
                gather.rows("low nigh", 0, a, jnp.where(has_low & (sub < 1), c[5], 0.0))
            else:
                gather.rows("high far", 1, a, jnp.where(has_high, c[7], 0.0))
                gather.rows("high nigh", 1, a, jnp.where(has_high & (sub >= SUB - 1), c[6], 0.0))
    for i, name in enumerate(("outer", "inner")):
        for half in range(2):
            cols_ref[i, half_rows(half), :] = gather.got[name, half]
    for i, name in enumerate(("low far", "low nigh", "high far", "high nigh")):
        for q in range(na // 4):
            rows_ref[i, half_rows(q), :] = gather.got[name, q]


def donor_at(at):
    return jnp.where(at < 0, at + lax.axis_size("circ"), at)


def add_tiles(x, sources, placed_ref, s, a, half, nv):
    for tile_ref, start, donor in sources:
        for t in range(placed_ref.shape[1]):
            at = start + (t * nv + s) * 2 + a
            tile = jnp.broadcast_to(tile_ref[at : at + 1, :], (SUB, LANES))
            x = x + placed_ref[donor, t, half_rows(half), :] * tile
    return x


def local_kernel(tiles, *refs):
    lam_ref, couple_ref, jac_ref, rhs_ref, inv_ref = refs[:5]
    nv, na = lam_ref.shape[:2]
    sub, lane = iotas()
    if tiles:
        placed_ref, *tile_refs, base_ref, sum_ref = refs[5:]
        me = lax.axis_index("circ")
        sources = [(ref, 0, donor_at(me - 2 * n)) for n, ref in enumerate(tile_refs)]
    else:
        base_ref = refs[5]
    for a in range(na):
        coef = [
            inner_coefs([couple_ref[i, a, half_rows(h), :] for i in range(12)], h, sub, lane) for h in range(2)
        ]
        near = local_sums(lam_ref, a, coef, sub)
        for half in range(2):
            inv = inv_ref[a, half_rows(half), :]
            for s in range(nv):
                acc = rhs_ref[s, a, half_rows(half), :]
                if tiles:
                    if a < 2:
                        acc = add_tiles(acc, sources, placed_ref, s, a, half, nv)
                    sum_ref[s, a, half_rows(half), :] = acc
                for b in range(nv):
                    acc = acc + jac_ref[s, b, a, half_rows(half), :] * near[b][half]
                base_ref[s, a, half_rows(half), :] = acc * inv


def relay_kernel(first, cols_ref, tile_ref, _, out_ref, *, share):
    half = out_ref.shape[0] - share
    out_ref[share:, :] = tile_ref[half : 2 * half, :]
    if first < cols_ref.shape[0]:
        out_ref[:share, :] = cols_ref[first : first + share, :]


def shares(routes):
    return SUB * max(1, 2 // routes)


def halo_sums(nv, na, ahead_ref, back_ref, across_ref, mate_at, cols_ref, rows_ref):
    sub, lane = iotas()
    me, rad = lax.axis_index("circ"), lax.axis_index("rad")
    out = []
    right, left = [], []
    for half in range(2):
        x, y = mate_at(half), across_ref[half_rows(half), :]
        right.append(jnp.where(me % 2 == 0, x, y))
        left.append(jnp.where(me % 2 == 0, y, x))
    for v in range(nv):
        _, spot = slot(v, 0, na)
        cols = []
        for half in range(2):
            r, l = right[half], left[half]
            wide = jnp.where(lane % 4 < 2, along(r, -spot - 2), along(l, 2 - spot))
            slim = jnp.where(lane % 4 < 2, along(r, -spot - 1), along(l, 1 - spot))
            cols.append(cols_ref[0, half_rows(half), :] * wide + cols_ref[1, half_rows(half), :] * slim)
        low, high = [], []
        for q in range(na // 4):
            rows = half_rows(v * (na // 4) + q)
            x, y = ahead_ref[rows, :], back_ref[rows, :]
            m, p = jnp.where(rad % 2 == 0, y, x), jnp.where(rad % 2 == 0, x, y)
            low.append(rows_ref[0, half_rows(q), :] * m + rows_ref[1, half_rows(q), :] * down(m, -1))
            high.append(rows_ref[2, half_rows(q), :] * p + rows_ref[3, half_rows(q), :] * down(p, 1))
        out.append((cols, low, high))
    return out


def spread(x, part, a, half, sub, lane):
    cols, low, high = part
    x = x + jnp.where((lane < 2) | (lane >= LANES - 2), along(cols[half], LANES - 2 - 4 * a), 0.0)
    j = a % 4
    if half == 0:
        return x + jnp.where(sub < 2, down(low[a // 4], -2 * j), 0.0)
    return x + jnp.where(sub >= SUB - 2, down(high[a // 4], SUB - 2 - 2 * j), 0.0)


def finish_kernel(routes, last, *refs):
    base_ref, cols_ref, rows_ref, edge_cols, edge_low, edge_high, ahead_ref, back_ref, across_ref = refs[:9]
    nv, na = base_ref.shape[:2]
    sub, lane = iotas()
    if routes:
        rhs_ref, inv_ref, placed_ref, *relayed = refs[9 : 12 + routes]
        out_ref, sum_ref, *rest = refs[12 + routes :]
        share = shares(routes)
        mate_at = lambda half: relayed[SUB * half // share][SUB * half % share : SUB * half % share + SUB, :]
        me = lax.axis_index("circ")
        sources = [(ref, share, donor_at(me + 1 - 2 * (me % 2) - 2 * n)) for n, ref in enumerate(relayed)]
    else:
        mate_ref, out_ref, *rest = refs[9:]
        mate_at = lambda half: mate_ref[half_rows(half), :]
    if last:
        result_ref, out_ref, sems = out_ref, *rest
        copies = []
    sums = halo_sums(nv, na, ahead_ref, back_ref, across_ref, mate_at, cols_ref, rows_ref)
    parts = []
    for s in range(nv):
        turned = []
        for kind, edge_ref in enumerate((edge_cols, edge_low, edge_high)):
            turned.append([])
            for q in range(2 if kind == 0 else na // 4):
                total = edge_ref[s, 0, half_rows(q), :] * sums[0][kind][q]
                for b in range(1, nv):
                    total = total + edge_ref[s, b, half_rows(q), :] * sums[b][kind][q]
                turned[-1].append(total)
        parts.append(turned)
    packer = None if last else Packer(na, nv)
    for a in range(na):
        for half in range(2):
            for s in range(nv):
                x = spread(base_ref[s, a, half_rows(half), :], parts[s], a, half, sub, lane)
                if routes:
                    total = rhs_ref[s, a, half_rows(half), :]
                    if a < 2:
                        more = add_tiles(jnp.zeros_like(x), sources, placed_ref, s, a, half, nv)
                        total = total + more
                        x = x + more * inv_ref[a, half_rows(half), :]
                    sum_ref[s, a, half_rows(half), :] = total
                out_ref[s, a, half_rows(half), :] = x
                if packer is not None:
                    packer.add(s, a, half, x)
        if last:
            copy = pltpu.make_async_copy(out_ref.at[:, a], result_ref.at[:, a], sems.at[a])
            copy.start()
            copies.append(copy)
    if last:
        for copy in copies:
            copy.wait()
    else:
        ahead_to, back_to, across_to, mate_to = rest
        packer.write(ahead_to, back_to, across_to, [mate_to.at[:SUB], mate_to.at[SUB:]])


def call(kernel, name, outs, args, specs=None, scratch=(), us=1, out_specs=None):
    vmem = pl.BlockSpec(memory_space=pltpu.VMEM)
    return pl.pallas_call(
        kernel,
        out_shape=outs,
        in_specs=[vmem] * len(args) if specs is None else specs,
        out_specs=[vmem] * len(outs) if out_specs is None else out_specs,
        scratch_shapes=list(scratch),
        compiler_params=PARAMS,
        cost_estimate=pl.CostEstimate(
            flops=us * 1_000_000, bytes_accessed=us * 3_000_000, transcendentals=0
        ),
        name=name,
    )(*args)


def solution(mesh):
    route = routes(mesh)
    vmem = lambda *shape: pltpu.VMEM(shape, jnp.float32)
    inside = pl.BlockSpec(memory_space=pltpu.VMEM)
    outside = pl.BlockSpec(memory_space=pltpu.HBM)
    unread = pl.BlockSpec(memory_space=pl.ANY)
    far = lambda x: pltpu.with_memory_space_constraint(x, pltpu.HBM)

    def sent(x, pairs):
        return lax.ppermute(x, AXES, pairs)

    def per_device(adjoint, source, jacobian, couple, donor_row, target_row, tile_count, weights):
        nv, na, nr, nc = adjoint.shape[1:]
        donors, slots = donor_row.shape[2:]
        count = len(route["faces"])
        sides = 2 * nv * na
        edges = lambda across: [vmem(sides + SUB, nc), vmem(sides, nc), vmem(across, nc), vmem(nr, nc)]
        block = vmem(nv, na, nr, nc)
        lam, cpl, rhs, *tiles = call(
            load_kernel, "load",
            [block, vmem(12, na, nr, nc), block] + [vmem(4 * slots * nv + SUB * n, nc) for n in range(count)],
            [*map(far, (adjoint[0], donor_row[0], couple[0], source[0]))], [outside] * 4,
            [pltpu.SMEM(donor_row.shape[1:], jnp.int32), pltpu.SemaphoreType.DMA((4,))],
        )
        ahead, back, cross, cols = call(pack_kernel, "pack", edges(sides - SUB), [lam])
        tiles = [sent(x, pairs) for x, pairs in zip(tiles, route["faces"])]
        for sweep in range(SWEEPS):
            last = sweep == SWEEPS - 1
            ahead = sent(ahead, route["ahead"])
            back = sent(back, route["back"])
            across = sent(cross, route["across"])
            if sweep == 0:
                share = shares(count)
                jac, placed, inv, edge_coefs, row_coefs, *matrices = call(
                    fetch_kernel, "fetch",
                    [vmem(nv, nv, na, nr, nc), vmem(donors, slots, nr, nc), vmem(na, nr, nc),
                     vmem(2, nr, nc), vmem(4, 2 * na, nc), vmem(nv, nv, nr, nc)] + [vmem(nv, nv, 2 * na, nc)] * 2,
                    [cpl, *map(far, (jacobian[0], target_row[0], tile_count[0], weights.reshape(-1, nc)))],
                    [inside] + [outside] * 4,
                    [pltpu.SMEM(target_row.shape[1:], jnp.int32), pltpu.SMEM(tile_count.shape[1:], jnp.int32),
                     pltpu.VMEM((donors * slots, nc), jnp.float32), pltpu.SemaphoreType.DMA((nv + 3,))],
                )
                relayed = [
                    call(functools.partial(relay_kernel, share * n, share=share), f"relay{n}",
                         [vmem(share + 2 * slots * nv, nc)], [cols, x, inv], [inside] * 2 + [unread])[0]
                    for n, x in enumerate(tiles)
                ]
                relayed = [sent(x, route["mate"]) for x in relayed]
                base, rhs = call(
                    functools.partial(local_kernel, True), "local0", [block] * 2, [lam, cpl, jac, rhs, inv, placed, *tiles]
                )
                lam, rhs, ahead, back, cross, cols = call(
                    functools.partial(finish_kernel, count, False), "finish0", [block] * 2 + edges(nr + SUB),
                    [base, edge_coefs, row_coefs, *matrices, ahead, back, across, rhs, inv, placed, *relayed],
                )
                continue
            mate = sent(cols, route["mate"])
            base = call(
                functools.partial(local_kernel, False), f"local{sweep}", [block], [lam, cpl, jac, rhs, inv]
            )[0]
            scratch, spaces, outs = [], None, [block] + edges(nr + SUB)
            if last:
                outs, spaces = [jax.ShapeDtypeStruct((nv, na, nr, nc), jnp.float32)], [outside]
                scratch = [pltpu.VMEM((nv, na, nr, nc), jnp.float32), pltpu.SemaphoreType.DMA((na,))]
            lam, *more = call(
                functools.partial(finish_kernel, 0, last), f"finish{sweep}", outs,
                [base, edge_coefs, row_coefs, *matrices, ahead, back, across, mate], None, scratch, 1, spaces,
            )
            if not last:
                ahead, back, cross, cols = more
        return lam[None]

    in_specs = (
        P("sec", None, None, "rad", "circ"),
        P("sec", None, None, "rad", "circ"),
        P("sec", None, None, None, "rad", "circ"),
        P("sec", None, None, "rad", "circ"),
        P("rad", None, None, None),
        P("rad", None, None, None),
        P("rad", None, None),
        P("rad", None, "circ", None, None),
    )
    out_specs = P("sec", None, None, "rad", "circ")
    return jax.shard_map(
        per_device, mesh=mesh, in_specs=in_specs, out_specs=out_specs, check_vma=False
    )
```

```python
import functools

import jax
import jax.numpy as jnp
from jax import lax
from jax.experimental import pallas as pl
from jax.experimental.pallas import tpu as pltpu
from jax.sharding import PartitionSpec as P

SWEEPS = 3
AXES = ("sec", "circ", "rad")
SUB, LANES = 8, 128
PARAMS = pltpu.CompilerParams(vmem_limit_bytes=16 * 1024 * 1024)


def routes(mesh):
    secs, circs, rads = (mesh.shape[a] for a in AXES)

    def pairs(target):
        flat = lambda s, c, r: (s * circs + c) * rads + r
        return [
            (flat(s, c, r), flat(*target(s, c, r)))
            for s in range(secs)
            for c in range(circs)
            for r in range(rads)
        ]

    def swap(s, c, r, odd):
        q = r + 1 if (r + odd) % 2 == 0 else r - 1
        return (s, c, q) if 0 <= q < rads else (s, c ^ 1, r)

    return {
        "ahead": pairs(lambda s, c, r: swap(s, c, r, 0)),
        "back": pairs(lambda s, c, r: swap(s, c, r, 1)),
        "mate": pairs(lambda s, c, r: (s, c ^ 1, r)),
        "across": pairs(lambda s, c, r: (s, (c - 1 if c % 2 == 0 else c + 1) % circs, r)),
        "faces": [
            pairs(lambda s, c, r: (1, (c + k) % circs, r) if s == 0 else (0, (c - k) % circs, r))
            for k in range(0, circs, 2)
        ],
    }


def iotas():
    sub = lax.broadcasted_iota(jnp.int32, (SUB, LANES), 0)
    lane = lax.broadcasted_iota(jnp.int32, (SUB, LANES), 1)
    return sub, lane


def down(x, by):
    return pltpu.roll(x, by % SUB, 0) if by % SUB else x


def along(x, by):
    return pltpu.roll(x, by % LANES, 1) if by % LANES else x


def half_rows(half):
    return slice(SUB * half, SUB * (half + 1))


def slot(v, a, na):
    return v % 2, 4 * (na * (v // 2) + a) + 2 * (v % 2)


class Packer:
    def __init__(self, na, nv):
        self.sub, self.lane = iotas()
        self.na = na
        self.low, self.high, self.cols = {}, {}, {}

    def put(self, book, key, keep, x):
        book[key] = jnp.where(keep, x, book[key]) if key in book else x

    def add(self, v, a, half, x):
        k = v * self.na + a
        group, j = k // 4, k % 4
        inside = (self.sub >= 2 * j) & (self.sub < 2 * j + 2)
        if half == 0:
            self.put(self.low, group, inside, down(x, 2 * j))
        else:
            self.put(self.high, group, inside, down(x, 2 * j + 2))
        part, spot = slot(v, a, self.na)
        inside = (self.lane >= spot) & (self.lane < spot + 4)
        self.put(self.cols, (part, half), inside, along(x, spot + 2))

    def write(self, ahead_ref, back_ref, across_ref, mate_refs):
        even = lax.axis_index("rad") % 2 == 0
        for g in range(len(self.low)):
            rows = slice(SUB * g, SUB * (g + 1))
            ahead_ref[rows, :] = jnp.where(even, self.high[g], self.low[g])
            back_ref[rows, :] = jnp.where(even, self.low[g], self.high[g])
        even = lax.axis_index("circ") % 2 == 0
        for half in range(2):
            x, y = self.cols[0, half], self.cols[1, half]
            right = jnp.where(self.lane % 4 < 2, x, y)
            left = jnp.where(self.lane % 4 < 2, y, x)
            rows = slice(SUB * half, SUB * (half + 1))
            across_ref[rows, :] = jnp.where(even, left, right)
            mate_refs[half][...] = jnp.where(even, right, left)


def pack_kernel(lam_ref, ahead_ref, back_ref, across_ref, mate_ref):
    nv, na = lam_ref.shape[:2]
    packer = Packer(na, nv)
    for a in range(na):
        for v in range(nv):
            for half in range(2):
                packer.add(v, a, half, lam_ref[v, a, SUB * half : SUB * (half + 1), :])
    packer.write(ahead_ref, back_ref, across_ref, [mate_ref.at[:SUB], mate_ref.at[SUB:]])


def fetch_kernel(couple_ref, jac_in, targets_in, counts_in, weights_in, *refs):
    jac_ref, placed_ref, inv_ref, cols_ref, rows_ref, *edge_refs = refs[:8]
    targets_ref, counts_ref, weights_ref, sems = refs[8:]
    count = jac_ref.shape[0]
    slim = [
        pltpu.make_async_copy(targets_in, targets_ref, sems.at[count]),
        pltpu.make_async_copy(counts_in, counts_ref, sems.at[count + 1]),
        pltpu.make_async_copy(weights_in, weights_ref, sems.at[count + 2]),
    ]
    wide = [pltpu.make_async_copy(jac_in.at[s], jac_ref.at[s], sems.at[s]) for s in range(count)]
    for copy in slim + wide:
        copy.start()
    coefs_of(couple_ref, inv_ref, cols_ref, rows_ref)
    for copy in slim:
        copy.wait()
    place_weights(targets_ref, counts_ref, weights_ref, placed_ref)
    for s, copy in enumerate(wide):
        copy.wait()
        edge_matrices(s, jac_ref, inv_ref, *edge_refs)


def edge_matrices(s, jac_ref, inv_ref, cols_ref, low_ref, high_ref):
    nv, na = jac_ref.shape[1:3]
    sub, lane = iotas()
    for b in range(nv):
        gather = Gather(sub, lane)
        for a in range(na):
            for half in range(2):
                m = jac_ref[s, b, a, half_rows(half), :] * inv_ref[a, half_rows(half), :]
                gather.cols("cols", half, a, m)
                gather.rows("high" if half else "low", half, a, m)
        for half in range(2):
            cols_ref[s, b, half_rows(half), :] = gather.got["cols", half]
        for q in range(na // 4):
            low_ref[s, b, half_rows(q), :] = gather.got["low", q]
            high_ref[s, b, half_rows(q), :] = gather.got["high", q]


def load_kernel(adjoint_ref, donors_in, couple_in, src_in, *refs):
    lam_ref, couple_ref, src_ref, *tile_refs, donors_ref, sems = refs
    nv, na, nr, _ = lam_ref.shape
    copies = [
        pltpu.make_async_copy(donors_in, donors_ref, sems.at[0]),
        pltpu.make_async_copy(adjoint_ref, lam_ref, sems.at[1]),
        pltpu.make_async_copy(couple_in, couple_ref, sems.at[2]),
        pltpu.make_async_copy(src_in, src_ref, sems.at[3]),
    ]
    for copy in copies:
        copy.start()
    copies[0].wait()
    copies[1].wait()
    me, circs, slots = lax.axis_index("circ"), donors_ref.shape[1], donors_ref.shape[2]
    for n, tile_ref in enumerate(tile_refs):
        reader = jnp.where(me + 2 * n >= circs, me + 2 * n - circs, me + 2 * n)
        for part, to in enumerate((reader, reader + 1 - 2 * (reader % 2))):
            for k in range(slots):
                row = jnp.clip(donors_ref[me, to, k], 0, nr - 1)
                for v in range(nv):
                    for a in range(2):
                        at = ((part * slots + k) * nv + v) * 2 + a
                        tile_ref[at : at + 1, :] = lam_ref[v, na - 2 + a, pl.ds(row, 1), :]
    for copy in copies[2:]:
        copy.wait()


def place_weights(targets_ref, counts_ref, weights_ref, placed_ref):
    me = lax.axis_index("circ")
    stator = lax.axis_index("sec") == 1
    sub, _ = iotas()
    slots = targets_ref.shape[-1]
    for d in range(targets_ref.shape[0]):
        for k in range(slots):
            live = (k < counts_ref[d, me]) & stator
            row = jnp.where(live, targets_ref[d, me, k], -1)
            w = jnp.broadcast_to(weights_ref[d * slots + k : d * slots + k + 1, :], (SUB, LANES))
            for h in range(2):
                placed_ref[d, k, SUB * h : SUB * (h + 1), :] = jnp.where(sub + SUB * h == row, w, 0.0)


def inner_coefs(c, half, sub, lane):
    c = list(c)
    if half == 0:
        c[4] = jnp.where(sub >= 2, c[4], 0.0)
        c[5] = jnp.where(sub >= 1, c[5], 0.0)
    else:
        c[6] = jnp.where(sub < SUB - 1, c[6], 0.0)
        c[7] = jnp.where(sub < SUB - 2, c[7], 0.0)
    c[8] = jnp.where(lane >= 2, c[8], 0.0)
    c[9] = jnp.where(lane >= 1, c[9], 0.0)
    c[10] = jnp.where(lane < LANES - 1, c[10], 0.0)
    c[11] = jnp.where(lane < LANES - 2, c[11], 0.0)
    return c


def local_sums(lam_ref, a, coef, sub):
    nv, na = lam_ref.shape[:2]
    sums = []
    for v in range(nv):
        x = [lam_ref[v, a, half_rows(h), :] for h in range(2)]
        moved = {o: [down(x[h], -o) for h in range(2)] for o in (-2, -1, 1, 2)}
        both = []
        for half in range(2):
            c = coef[half]
            total = None
            for i, o in enumerate((-2, -1, 1, 2)):
                if 0 <= a + o < na:
                    term = c[i] * lam_ref[v, a + o, half_rows(half), :]
                    total = term if total is None else total + term
            for i, o in enumerate((-2, -1, 1, 2)):
                m = moved[o]
                if o < 0:
                    y = m[0] if half == 0 else jnp.where(sub >= -o, m[1], m[0])
                else:
                    y = m[1] if half == 1 else jnp.where(sub < SUB - o, m[0], m[1])
                total = total + c[4 + i] * y
            for i, o in enumerate((-2, -1, 1, 2)):
                total = total + c[8 + i] * along(x[half], -o)
            both.append(total)
        sums.append(both)
    return sums


class Gather:
    def __init__(self, sub, lane):
        self.sub, self.lane = sub, lane
        self.got = {}

    def put(self, key, keep, x):
        self.got[key] = jnp.where(keep, x, self.got[key]) if key in self.got else x

    def cols(self, name, half, a, x):
        inside = (self.lane >= 4 * a) & (self.lane < 4 * a + 4)
        self.put((name, half), inside, along(x, 4 * a + 2))

    def rows(self, name, half, a, x):
        j = a % 4
        inside = (self.sub >= 2 * j) & (self.sub < 2 * j + 2)
        self.put((name, a // 4), inside, down(x, 2 * j + 2 * half))


def coefs_of(couple_ref, inv_ref, cols_ref, rows_ref):
    na = couple_ref.shape[1]
    sub, lane = iotas()
    rad = lax.axis_index("rad")
    has_low, has_high = rad > 0, rad < lax.axis_size("rad") - 1
    gather = Gather(sub, lane)
    for a in range(na):
        for half in range(2):
            c = [couple_ref[i, a, half_rows(half), :] for i in range(12)]
            total = c[0]
            for i in range(1, 12):
                total = total + c[i]
            inv_ref[a, half_rows(half), :] = 1.0 / (1.0 + total)
            gather.cols("outer", half, a, jnp.where(lane < 2, c[8], jnp.where(lane >= LANES - 2, c[11], 0.0)))
            gather.cols("inner", half, a, jnp.where(lane < 1, c[9], jnp.where(lane >= LANES - 1, c[10], 0.0)))
            if half == 0:
                gather.rows("low far", 0, a, jnp.where(has_low, c[4], 0.0))
                gather.rows("low nigh", 0, a, jnp.where(has_low & (sub < 1), c[5], 0.0))
            else:
                gather.rows("high far", 1, a, jnp.where(has_high, c[7], 0.0))
                gather.rows("high nigh", 1, a, jnp.where(has_high & (sub >= SUB - 1), c[6], 0.0))
    for i, name in enumerate(("outer", "inner")):
        for half in range(2):
            cols_ref[i, half_rows(half), :] = gather.got[name, half]
    for i, name in enumerate(("low far", "low nigh", "high far", "high nigh")):
        for q in range(na // 4):
            rows_ref[i, half_rows(q), :] = gather.got[name, q]


def donor_at(at):
    return jnp.where(at < 0, at + lax.axis_size("circ"), at)


def add_tiles(x, sources, placed_ref, s, a, half, nv):
    for tile_ref, start, donor in sources:
        for t in range(placed_ref.shape[1]):
            at = start + (t * nv + s) * 2 + a
            tile = jnp.broadcast_to(tile_ref[at : at + 1, :], (SUB, LANES))
            x = x + placed_ref[donor, t, half_rows(half), :] * tile
    return x


def local_kernel(tiles, *refs):
    lam_ref, couple_ref, jac_ref, rhs_ref, inv_ref = refs[:5]
    nv, na = lam_ref.shape[:2]
    sub, lane = iotas()
    if tiles:
        placed_ref, *tile_refs, base_ref, sum_ref = refs[5:]
        me = lax.axis_index("circ")
        sources = [(ref, 0, donor_at(me - 2 * n)) for n, ref in enumerate(tile_refs)]
    else:
        base_ref = refs[5]
    for a in range(na):
        coef = [
            inner_coefs([couple_ref[i, a, half_rows(h), :] for i in range(12)], h, sub, lane) for h in range(2)
        ]
        near = local_sums(lam_ref, a, coef, sub)
        for half in range(2):
            inv = inv_ref[a, half_rows(half), :]
            for s in range(nv):
                acc = rhs_ref[s, a, half_rows(half), :]
                if tiles:
                    if a < 2:
                        acc = add_tiles(acc, sources, placed_ref, s, a, half, nv)
                    sum_ref[s, a, half_rows(half), :] = acc
                for b in range(nv):
                    acc = acc + jac_ref[s, b, a, half_rows(half), :] * near[b][half]
                base_ref[s, a, half_rows(half), :] = acc * inv


def relay_kernel(first, cols_ref, tile_ref, _, out_ref, *, share):
    half = out_ref.shape[0] - share
    out_ref[share:, :] = tile_ref[half : 2 * half, :]
    if first < cols_ref.shape[0]:
        out_ref[:share, :] = cols_ref[first : first + share, :]


def shares(routes):
    return SUB * max(1, 2 // routes)


def halo_sums(nv, na, ahead_ref, back_ref, across_ref, mate_at, cols_ref, rows_ref):
    sub, lane = iotas()
    me, rad = lax.axis_index("circ"), lax.axis_index("rad")
    out = []
    right, left = [], []
    for half in range(2):
        x, y = mate_at(half), across_ref[half_rows(half), :]
        right.append(jnp.where(me % 2 == 0, x, y))
        left.append(jnp.where(me % 2 == 0, y, x))
    for v in range(nv):
        _, spot = slot(v, 0, na)
        cols = []
        for half in range(2):
            r, l = right[half], left[half]
            wide = jnp.where(lane % 4 < 2, along(r, -spot - 2), along(l, 2 - spot))
            slim = jnp.where(lane % 4 < 2, along(r, -spot - 1), along(l, 1 - spot))
            cols.append(cols_ref[0, half_rows(half), :] * wide + cols_ref[1, half_rows(half), :] * slim)
        low, high = [], []
        for q in range(na // 4):
            rows = half_rows(v * (na // 4) + q)
            x, y = ahead_ref[rows, :], back_ref[rows, :]
            m, p = jnp.where(rad % 2 == 0, y, x), jnp.where(rad % 2 == 0, x, y)
            low.append(rows_ref[0, half_rows(q), :] * m + rows_ref[1, half_rows(q), :] * down(m, -1))
            high.append(rows_ref[2, half_rows(q), :] * p + rows_ref[3, half_rows(q), :] * down(p, 1))
        out.append((cols, low, high))
    return out


def spread(x, part, a, half, sub, lane):
    cols, low, high = part
    x = x + jnp.where((lane < 2) | (lane >= LANES - 2), along(cols[half], LANES - 2 - 4 * a), 0.0)
    j = a % 4
    if half == 0:
        return x + jnp.where(sub < 2, down(low[a // 4], -2 * j), 0.0)
    return x + jnp.where(sub >= SUB - 2, down(high[a // 4], SUB - 2 - 2 * j), 0.0)


def finish_kernel(routes, last, *refs):
    base_ref, cols_ref, rows_ref, edge_cols, edge_low, edge_high, ahead_ref, back_ref, across_ref = refs[:9]
    nv, na = base_ref.shape[:2]
    sub, lane = iotas()
    if routes:
        rhs_ref, inv_ref, placed_ref, *relayed = refs[9 : 12 + routes]
        out_ref, sum_ref, *rest = refs[12 + routes :]
        share = shares(routes)
        mate_at = lambda half: relayed[SUB * half // share][SUB * half % share : SUB * half % share + SUB, :]
        me = lax.axis_index("circ")
        sources = [(ref, share, donor_at(me + 1 - 2 * (me % 2) - 2 * n)) for n, ref in enumerate(relayed)]
    else:
        mate_ref, out_ref, *rest = refs[9:]
        mate_at = lambda half: mate_ref[half_rows(half), :]
    if last:
        result_ref, out_ref, sems = out_ref, *rest
        copies = []
    sums = halo_sums(nv, na, ahead_ref, back_ref, across_ref, mate_at, cols_ref, rows_ref)
    packer = None if last else Packer(na, nv)
    for s in range(nv):
        turned = []
        for kind, edge_ref in enumerate((edge_cols, edge_low, edge_high)):
            turned.append([])
            for q in range(2 if kind == 0 else na // 4):
                total = edge_ref[s, 0, half_rows(q), :] * sums[0][kind][q]
                for b in range(1, nv):
                    total = total + edge_ref[s, b, half_rows(q), :] * sums[b][kind][q]
                turned[-1].append(total)
        for a in range(na):
            for half in range(2):
                x = spread(base_ref[s, a, half_rows(half), :], turned, a, half, sub, lane)
                if routes:
                    total = rhs_ref[s, a, half_rows(half), :]
                    if a < 2:
                        more = add_tiles(jnp.zeros_like(x), sources, placed_ref, s, a, half, nv)
                        total = total + more
                        x = x + more * inv_ref[a, half_rows(half), :]
                    sum_ref[s, a, half_rows(half), :] = total
                out_ref[s, a, half_rows(half), :] = x
                if packer is not None:
                    packer.add(s, a, half, x)
        if last:
            copy = pltpu.make_async_copy(out_ref.at[s], result_ref.at[s], sems.at[s])
            copy.start()
            copies.append(copy)
    if last:
        for copy in copies:
            copy.wait()
    else:
        ahead_to, back_to, across_to, mate_to = rest
        packer.write(ahead_to, back_to, across_to, [mate_to.at[:SUB], mate_to.at[SUB:]])


def call(kernel, name, outs, args, specs=None, scratch=(), us=1, out_specs=None):
    vmem = pl.BlockSpec(memory_space=pltpu.VMEM)
    return pl.pallas_call(
        kernel,
        out_shape=outs,
        in_specs=[vmem] * len(args) if specs is None else specs,
        out_specs=[vmem] * len(outs) if out_specs is None else out_specs,
        scratch_shapes=list(scratch),
        compiler_params=PARAMS,
        cost_estimate=pl.CostEstimate(
            flops=us * 1_000_000, bytes_accessed=us * 3_000_000, transcendentals=0
        ),
        name=name,
    )(*args)


def solution(mesh):
    route = routes(mesh)
    vmem = lambda *shape: pltpu.VMEM(shape, jnp.float32)
    inside = pl.BlockSpec(memory_space=pltpu.VMEM)
    outside = pl.BlockSpec(memory_space=pltpu.HBM)
    unread = pl.BlockSpec(memory_space=pl.ANY)
    far = lambda x: pltpu.with_memory_space_constraint(x, pltpu.HBM)

    def sent(x, pairs):
        return lax.ppermute(x, AXES, pairs)

    def per_device(adjoint, source, jacobian, couple, donor_row, target_row, tile_count, weights):
        nv, na, nr, nc = adjoint.shape[1:]
        donors, slots = donor_row.shape[2:]
        count = len(route["faces"])
        sides = 2 * nv * na
        edges = lambda across: [vmem(sides + SUB, nc), vmem(sides, nc), vmem(across, nc), vmem(nr, nc)]
        block = vmem(nv, na, nr, nc)
        lam, cpl, rhs, *tiles = call(
            load_kernel, "load",
            [block, vmem(12, na, nr, nc), block] + [vmem(4 * slots * nv + SUB * n, nc) for n in range(count)],
            [*map(far, (adjoint[0], donor_row[0], couple[0], source[0]))], [outside] * 4,
            [pltpu.SMEM(donor_row.shape[1:], jnp.int32), pltpu.SemaphoreType.DMA((4,))],
        )
        ahead, back, cross, cols = call(pack_kernel, "pack", edges(sides - SUB), [lam])
        tiles = [sent(x, pairs) for x, pairs in zip(tiles, route["faces"])]
        for sweep in range(SWEEPS):
            last = sweep == SWEEPS - 1
            ahead = sent(ahead, route["ahead"])
            back = sent(back, route["back"])
            across = sent(cross, route["across"])
            if sweep == 0:
                share = shares(count)
                jac, placed, inv, edge_coefs, row_coefs, *matrices = call(
                    fetch_kernel, "fetch",
                    [vmem(nv, nv, na, nr, nc), vmem(donors, slots, nr, nc), vmem(na, nr, nc),
                     vmem(2, nr, nc), vmem(4, 2 * na, nc), vmem(nv, nv, nr, nc)] + [vmem(nv, nv, 2 * na, nc)] * 2,
                    [cpl, *map(far, (jacobian[0], target_row[0], tile_count[0], weights.reshape(-1, nc)))],
                    [inside] + [outside] * 4,
                    [pltpu.SMEM(target_row.shape[1:], jnp.int32), pltpu.SMEM(tile_count.shape[1:], jnp.int32),
                     pltpu.VMEM((donors * slots, nc), jnp.float32), pltpu.SemaphoreType.DMA((nv + 3,))],
                )
                relayed = [
                    call(functools.partial(relay_kernel, share * n, share=share), f"relay{n}",
                         [vmem(share + 2 * slots * nv, nc)], [cols, x, inv], [inside] * 2 + [unread])[0]
                    for n, x in enumerate(tiles)
                ]
                relayed = [sent(x, route["mate"]) for x in relayed]
                base, rhs = call(
                    functools.partial(local_kernel, True), "local0", [block] * 2, [lam, cpl, jac, rhs, inv, placed, *tiles]
                )
                lam, rhs, ahead, back, cross, cols = call(
                    functools.partial(finish_kernel, count, False), "finish0", [block] * 2 + edges(nr + SUB),
                    [base, edge_coefs, row_coefs, *matrices, ahead, back, across, rhs, inv, placed, *relayed],
                )
                continue
            mate = sent(cols, route["mate"])
            base = call(
                functools.partial(local_kernel, False), f"local{sweep}", [block], [lam, cpl, jac, rhs, inv]
            )[0]
            scratch, spaces, outs = [], None, [block] + edges(nr + SUB)
            if last:
                outs, spaces = [jax.ShapeDtypeStruct((nv, na, nr, nc), jnp.float32)], [outside]
                scratch = [pltpu.VMEM((nv, na, nr, nc), jnp.float32), pltpu.SemaphoreType.DMA((nv,))]
            lam, *more = call(
                functools.partial(finish_kernel, 0, last), f"finish{sweep}", outs,
                [base, edge_coefs, row_coefs, *matrices, ahead, back, across, mate], None, scratch, 1, spaces,
            )
            if not last:
                ahead, back, cross, cols = more
        return lam[None]

    in_specs = (
        P("sec", None, None, "rad", "circ"),
        P("sec", None, None, "rad", "circ"),
        P("sec", None, None, None, "rad", "circ"),
        P("sec", None, None, "rad", "circ"),
        P("rad", None, None, None),
        P("rad", None, None, None),
        P("rad", None, None),
        P("rad", None, "circ", None, None),
    )
    out_specs = P("sec", None, None, "rad", "circ")
    return jax.shard_map(
        per_device, mesh=mesh, in_specs=in_specs, out_specs=out_specs, check_vma=False
    )
```

```python
import functools

import jax
import jax.numpy as jnp
from jax import lax
from jax.experimental import pallas as pl
from jax.experimental.pallas import tpu as pltpu
from jax.sharding import PartitionSpec as P

SWEEPS = 3
AXES = ("sec", "circ", "rad")
SUB, LANES = 8, 128
PARAMS = pltpu.CompilerParams(vmem_limit_bytes=16 * 1024 * 1024)


def routes(mesh):
    secs, circs, rads = (mesh.shape[a] for a in AXES)

    def pairs(target):
        flat = lambda s, c, r: (s * circs + c) * rads + r
        return [
            (flat(s, c, r), flat(*target(s, c, r)))
            for s in range(secs)
            for c in range(circs)
            for r in range(rads)
        ]

    def swap(s, c, r, odd):
        q = r + 1 if (r + odd) % 2 == 0 else r - 1
        return (s, c, q) if 0 <= q < rads else (s, c ^ 1, r)

    return {
        "ahead": pairs(lambda s, c, r: swap(s, c, r, 0)),
        "back": pairs(lambda s, c, r: swap(s, c, r, 1)),
        "mate": pairs(lambda s, c, r: (s, c ^ 1, r)),
        "across": pairs(lambda s, c, r: (s, (c - 1 if c % 2 == 0 else c + 1) % circs, r)),
        "faces": [
            pairs(lambda s, c, r: (1, (c + k) % circs, r) if s == 0 else (0, (c - k) % circs, r))
            for k in range(0, circs, 2)
        ],
    }


def iotas():
    sub = lax.broadcasted_iota(jnp.int32, (SUB, LANES), 0)
    lane = lax.broadcasted_iota(jnp.int32, (SUB, LANES), 1)
    return sub, lane


def down(x, by):
    return pltpu.roll(x, by % SUB, 0) if by % SUB else x


def along(x, by):
    return pltpu.roll(x, by % LANES, 1) if by % LANES else x


def half_rows(half):
    return slice(SUB * half, SUB * (half + 1))


def slot(v, a, na):
    return v % 2, 4 * (na * (v // 2) + a) + 2 * (v % 2)


class Packer:
    def __init__(self, na, nv):
        self.sub, self.lane = iotas()
        self.na = na
        self.low, self.high, self.cols = {}, {}, {}

    def put(self, book, key, keep, x):
        book[key] = jnp.where(keep, x, book[key]) if key in book else x

    def add(self, v, a, half, x):
        k = v * self.na + a
        group, j = k // 4, k % 4
        inside = (self.sub >= 2 * j) & (self.sub < 2 * j + 2)
        if half == 0:
            self.put(self.low, group, inside, down(x, 2 * j))
        else:
            self.put(self.high, group, inside, down(x, 2 * j + 2))
        part, spot = slot(v, a, self.na)
        inside = (self.lane >= spot) & (self.lane < spot + 4)
        self.put(self.cols, (part, half), inside, along(x, spot + 2))

    def write(self, ahead_ref, back_ref, across_ref, mate_refs):
        even = lax.axis_index("rad") % 2 == 0
        for g in range(len(self.low)):
            rows = slice(SUB * g, SUB * (g + 1))
            ahead_ref[rows, :] = jnp.where(even, self.high[g], self.low[g])
            back_ref[rows, :] = jnp.where(even, self.low[g], self.high[g])
        even = lax.axis_index("circ") % 2 == 0
        for half in range(2):
            x, y = self.cols[0, half], self.cols[1, half]
            right = jnp.where(self.lane % 4 < 2, x, y)
            left = jnp.where(self.lane % 4 < 2, y, x)
            rows = slice(SUB * half, SUB * (half + 1))
            across_ref[rows, :] = jnp.where(even, left, right)
            mate_refs[half][...] = jnp.where(even, right, left)


def pack_kernel(lam_ref, ahead_ref, back_ref, across_ref, mate_ref):
    nv, na = lam_ref.shape[:2]
    packer = Packer(na, nv)
    for a in range(na):
        for v in range(nv):
            for half in range(2):
                packer.add(v, a, half, lam_ref[v, a, SUB * half : SUB * (half + 1), :])
    packer.write(ahead_ref, back_ref, across_ref, [mate_ref.at[:SUB], mate_ref.at[SUB:]])


def fetch_kernel(couple_ref, jac_in, targets_in, counts_in, weights_in, *refs):
    jac_ref, placed_ref, inv_ref, cols_ref, rows_ref, *edge_refs = refs[:8]
    targets_ref, counts_ref, weights_ref, sems = refs[8:]
    count = jac_ref.shape[0]
    slim = [
        pltpu.make_async_copy(targets_in, targets_ref, sems.at[count]),
        pltpu.make_async_copy(counts_in, counts_ref, sems.at[count + 1]),
        pltpu.make_async_copy(weights_in, weights_ref, sems.at[count + 2]),
    ]
    wide = [pltpu.make_async_copy(jac_in.at[s], jac_ref.at[s], sems.at[s]) for s in range(count)]
    for copy in slim + wide:
        copy.start()
    coefs_of(couple_ref, inv_ref, cols_ref, rows_ref)
    for copy in slim:
        copy.wait()
    place_weights(targets_ref, counts_ref, weights_ref, placed_ref)
    for s, copy in enumerate(wide):
        copy.wait()
        if s < edge_refs[0].shape[0]:
            edge_matrices(s, s, jac_ref, inv_ref, *edge_refs)


def edge_matrices(s, at, jac_ref, inv_ref, cols_ref, low_ref, high_ref):
    nv, na = jac_ref.shape[1:3]
    sub, lane = iotas()
    for b in range(nv):
        gather = Gather(sub, lane)
        for a in range(na):
            for half in range(2):
                m = jac_ref[s, b, a, half_rows(half), :] * inv_ref[a, half_rows(half), :]
                gather.cols("cols", half, a, m)
                gather.rows("high" if half else "low", half, a, m)
        for half in range(2):
            cols_ref[at, b, half_rows(half), :] = gather.got["cols", half]
        for q in range(na // 4):
            low_ref[at, b, half_rows(q), :] = gather.got["low", q]
            high_ref[at, b, half_rows(q), :] = gather.got["high", q]


def load_kernel(adjoint_ref, donors_in, couple_in, src_in, *refs):
    lam_ref, couple_ref, src_ref, *tile_refs, donors_ref, sems = refs
    nv, na, nr, _ = lam_ref.shape
    copies = [
        pltpu.make_async_copy(donors_in, donors_ref, sems.at[0]),
        pltpu.make_async_copy(adjoint_ref, lam_ref, sems.at[1]),
        pltpu.make_async_copy(couple_in, couple_ref, sems.at[2]),
        pltpu.make_async_copy(src_in, src_ref, sems.at[3]),
    ]
    for copy in copies:
        copy.start()
    copies[0].wait()
    copies[1].wait()
    me, circs, slots = lax.axis_index("circ"), donors_ref.shape[1], donors_ref.shape[2]
    for n, tile_ref in enumerate(tile_refs):
        reader = jnp.where(me + 2 * n >= circs, me + 2 * n - circs, me + 2 * n)
        for part, to in enumerate((reader, reader + 1 - 2 * (reader % 2))):
            for k in range(slots):
                row = jnp.clip(donors_ref[me, to, k], 0, nr - 1)
                for v in range(nv):
                    for a in range(2):
                        at = ((part * slots + k) * nv + v) * 2 + a
                        tile_ref[at : at + 1, :] = lam_ref[v, na - 2 + a, pl.ds(row, 1), :]
    for copy in copies[2:]:
        copy.wait()


def place_weights(targets_ref, counts_ref, weights_ref, placed_ref):
    me = lax.axis_index("circ")
    stator = lax.axis_index("sec") == 1
    sub, _ = iotas()
    slots = targets_ref.shape[-1]
    for d in range(targets_ref.shape[0]):
        for k in range(slots):
            live = (k < counts_ref[d, me]) & stator
            row = jnp.where(live, targets_ref[d, me, k], -1)
            w = jnp.broadcast_to(weights_ref[d * slots + k : d * slots + k + 1, :], (SUB, LANES))
            for h in range(2):
                placed_ref[d, k, SUB * h : SUB * (h + 1), :] = jnp.where(sub + SUB * h == row, w, 0.0)


def inner_coefs(c, half, sub, lane):
    c = list(c)
    if half == 0:
        c[4] = jnp.where(sub >= 2, c[4], 0.0)
        c[5] = jnp.where(sub >= 1, c[5], 0.0)
    else:
        c[6] = jnp.where(sub < SUB - 1, c[6], 0.0)
        c[7] = jnp.where(sub < SUB - 2, c[7], 0.0)
    c[8] = jnp.where(lane >= 2, c[8], 0.0)
    c[9] = jnp.where(lane >= 1, c[9], 0.0)
    c[10] = jnp.where(lane < LANES - 1, c[10], 0.0)
    c[11] = jnp.where(lane < LANES - 2, c[11], 0.0)
    return c


def local_sums(lam_ref, a, coef, sub):
    nv, na = lam_ref.shape[:2]
    sums = []
    for v in range(nv):
        x = [lam_ref[v, a, half_rows(h), :] for h in range(2)]
        moved = {o: [down(x[h], -o) for h in range(2)] for o in (-2, -1, 1, 2)}
        both = []
        for half in range(2):
            c = coef[half]
            total = None
            for i, o in enumerate((-2, -1, 1, 2)):
                if 0 <= a + o < na:
                    term = c[i] * lam_ref[v, a + o, half_rows(half), :]
                    total = term if total is None else total + term
            for i, o in enumerate((-2, -1, 1, 2)):
                m = moved[o]
                if o < 0:
                    y = m[0] if half == 0 else jnp.where(sub >= -o, m[1], m[0])
                else:
                    y = m[1] if half == 1 else jnp.where(sub < SUB - o, m[0], m[1])
                total = total + c[4 + i] * y
            for i, o in enumerate((-2, -1, 1, 2)):
                total = total + c[8 + i] * along(x[half], -o)
            both.append(total)
        sums.append(both)
    return sums


class Gather:
    def __init__(self, sub, lane):
        self.sub, self.lane = sub, lane
        self.got = {}

    def put(self, key, keep, x):
        self.got[key] = jnp.where(keep, x, self.got[key]) if key in self.got else x

    def cols(self, name, half, a, x):
        inside = (self.lane >= 4 * a) & (self.lane < 4 * a + 4)
        self.put((name, half), inside, along(x, 4 * a + 2))

    def rows(self, name, half, a, x):
        j = a % 4
        inside = (self.sub >= 2 * j) & (self.sub < 2 * j + 2)
        self.put((name, a // 4), inside, down(x, 2 * j + 2 * half))


def coefs_of(couple_ref, inv_ref, cols_ref, rows_ref):
    na = couple_ref.shape[1]
    sub, lane = iotas()
    rad = lax.axis_index("rad")
    has_low, has_high = rad > 0, rad < lax.axis_size("rad") - 1
    gather = Gather(sub, lane)
    for a in range(na):
        for half in range(2):
            c = [couple_ref[i, a, half_rows(half), :] for i in range(12)]
            total = c[0]
            for i in range(1, 12):
                total = total + c[i]
            inv_ref[a, half_rows(half), :] = 1.0 / (1.0 + total)
            gather.cols("outer", half, a, jnp.where(lane < 2, c[8], jnp.where(lane >= LANES - 2, c[11], 0.0)))
            gather.cols("inner", half, a, jnp.where(lane < 1, c[9], jnp.where(lane >= LANES - 1, c[10], 0.0)))
            if half == 0:
                gather.rows("low far", 0, a, jnp.where(has_low, c[4], 0.0))
                gather.rows("low nigh", 0, a, jnp.where(has_low & (sub < 1), c[5], 0.0))
            else:
                gather.rows("high far", 1, a, jnp.where(has_high, c[7], 0.0))
                gather.rows("high nigh", 1, a, jnp.where(has_high & (sub >= SUB - 1), c[6], 0.0))
    for i, name in enumerate(("outer", "inner")):
        for half in range(2):
            cols_ref[i, half_rows(half), :] = gather.got[name, half]
    for i, name in enumerate(("low far", "low nigh", "high far", "high nigh")):
        for q in range(na // 4):
            rows_ref[i, half_rows(q), :] = gather.got[name, q]


def donor_at(at):
    return jnp.where(at < 0, at + lax.axis_size("circ"), at)


def add_tiles(x, sources, placed_ref, s, a, half, nv):
    for tile_ref, start, donor in sources:
        for t in range(placed_ref.shape[1]):
            at = start + (t * nv + s) * 2 + a
            tile = jnp.broadcast_to(tile_ref[at : at + 1, :], (SUB, LANES))
            x = x + placed_ref[donor, t, half_rows(half), :] * tile
    return x


def local_kernel(tiles, *refs):
    lam_ref, couple_ref, jac_ref, rhs_ref, inv_ref = refs[:5]
    nv, na = lam_ref.shape[:2]
    sub, lane = iotas()
    if tiles:
        placed_ref, *tile_refs, base_ref, sum_ref = refs[5:-3]
        rest = refs[-3:]
        for s in range(nv - rest[0].shape[0], nv):
            edge_matrices(s, s - nv + rest[0].shape[0], jac_ref, inv_ref, *rest)
        me = lax.axis_index("circ")
        sources = [(ref, 0, donor_at(me - 2 * n)) for n, ref in enumerate(tile_refs)]
    else:
        base_ref = refs[5]
    for a in range(na):
        coef = [
            inner_coefs([couple_ref[i, a, half_rows(h), :] for i in range(12)], h, sub, lane) for h in range(2)
        ]
        near = local_sums(lam_ref, a, coef, sub)
        for half in range(2):
            inv = inv_ref[a, half_rows(half), :]
            for s in range(nv):
                acc = rhs_ref[s, a, half_rows(half), :]
                if tiles:
                    if a < 2:
                        acc = add_tiles(acc, sources, placed_ref, s, a, half, nv)
                    sum_ref[s, a, half_rows(half), :] = acc
                for b in range(nv):
                    acc = acc + jac_ref[s, b, a, half_rows(half), :] * near[b][half]
                base_ref[s, a, half_rows(half), :] = acc * inv


def relay_kernel(first, cols_ref, tile_ref, _, out_ref, *, share):
    half = out_ref.shape[0] - share
    out_ref[share:, :] = tile_ref[half : 2 * half, :]
    if first < cols_ref.shape[0]:
        out_ref[:share, :] = cols_ref[first : first + share, :]


def shares(routes):
    return SUB * max(1, 2 // routes)


def halo_sums(nv, na, ahead_ref, back_ref, across_ref, mate_at, cols_ref, rows_ref):
    sub, lane = iotas()
    me, rad = lax.axis_index("circ"), lax.axis_index("rad")
    out = []
    right, left = [], []
    for half in range(2):
        x, y = mate_at(half), across_ref[half_rows(half), :]
        right.append(jnp.where(me % 2 == 0, x, y))
        left.append(jnp.where(me % 2 == 0, y, x))
    for v in range(nv):
        _, spot = slot(v, 0, na)
        cols = []
        for half in range(2):
            r, l = right[half], left[half]
            wide = jnp.where(lane % 4 < 2, along(r, -spot - 2), along(l, 2 - spot))
            slim = jnp.where(lane % 4 < 2, along(r, -spot - 1), along(l, 1 - spot))
            cols.append(cols_ref[0, half_rows(half), :] * wide + cols_ref[1, half_rows(half), :] * slim)
        low, high = [], []
        for q in range(na // 4):
            rows = half_rows(v * (na // 4) + q)
            x, y = ahead_ref[rows, :], back_ref[rows, :]
            m, p = jnp.where(rad % 2 == 0, y, x), jnp.where(rad % 2 == 0, x, y)
            low.append(rows_ref[0, half_rows(q), :] * m + rows_ref[1, half_rows(q), :] * down(m, -1))
            high.append(rows_ref[2, half_rows(q), :] * p + rows_ref[3, half_rows(q), :] * down(p, 1))
        out.append((cols, low, high))
    return out


def spread(x, part, a, half, sub, lane):
    cols, low, high = part
    x = x + jnp.where((lane < 2) | (lane >= LANES - 2), along(cols[half], LANES - 2 - 4 * a), 0.0)
    j = a % 4
    if half == 0:
        return x + jnp.where(sub < 2, down(low[a // 4], -2 * j), 0.0)
    return x + jnp.where(sub >= SUB - 2, down(high[a // 4], SUB - 2 - 2 * j), 0.0)


def finish_kernel(routes, last, *refs):
    base_ref, cols_ref, rows_ref, *edges = refs[:9]
    ahead_ref, back_ref, across_ref, *refs = refs[9:]
    pick = lambda s: (edges[:3], s) if s < edges[0].shape[0] else (edges[3:], s - edges[0].shape[0])
    nv, na = base_ref.shape[:2]
    sub, lane = iotas()
    if routes:
        rhs_ref, inv_ref, placed_ref, *relayed = refs[: 3 + routes]
        out_ref, sum_ref, *rest = refs[3 + routes :]
        share = shares(routes)
        mate_at = lambda half: relayed[SUB * half // share][SUB * half % share : SUB * half % share + SUB, :]
        me = lax.axis_index("circ")
        sources = [(ref, share, donor_at(me + 1 - 2 * (me % 2) - 2 * n)) for n, ref in enumerate(relayed)]
    else:
        mate_ref, out_ref, *rest = refs
        mate_at = lambda half: mate_ref[half_rows(half), :]
    if last:
        result_ref, out_ref, sems = out_ref, *rest
        copies = []
    sums = halo_sums(nv, na, ahead_ref, back_ref, across_ref, mate_at, cols_ref, rows_ref)
    packer = None if last else Packer(na, nv)
    for s in range(nv):
        turned = []
        for kind, edge_ref in enumerate(pick(s)[0]):
            turned.append([])
            for q in range(2 if kind == 0 else na // 4):
                total = edge_ref[pick(s)[1], 0, half_rows(q), :] * sums[0][kind][q]
                for b in range(1, nv):
                    total = total + edge_ref[pick(s)[1], b, half_rows(q), :] * sums[b][kind][q]
                turned[-1].append(total)
        for a in range(na):
            for half in range(2):
                x = spread(base_ref[s, a, half_rows(half), :], turned, a, half, sub, lane)
                if routes:
                    total = rhs_ref[s, a, half_rows(half), :]
                    if a < 2:
                        more = add_tiles(jnp.zeros_like(x), sources, placed_ref, s, a, half, nv)
                        total = total + more
                        x = x + more * inv_ref[a, half_rows(half), :]
                    sum_ref[s, a, half_rows(half), :] = total
                out_ref[s, a, half_rows(half), :] = x
                if packer is not None:
                    packer.add(s, a, half, x)
        if last:
            copy = pltpu.make_async_copy(out_ref.at[s], result_ref.at[s], sems.at[s])
            copy.start()
            copies.append(copy)
    if last:
        for copy in copies:
            copy.wait()
    else:
        ahead_to, back_to, across_to, mate_to = rest
        packer.write(ahead_to, back_to, across_to, [mate_to.at[:SUB], mate_to.at[SUB:]])


def call(kernel, name, outs, args, specs=None, scratch=(), us=1, out_specs=None):
    vmem = pl.BlockSpec(memory_space=pltpu.VMEM)
    return pl.pallas_call(
        kernel,
        out_shape=outs,
        in_specs=[vmem] * len(args) if specs is None else specs,
        out_specs=[vmem] * len(outs) if out_specs is None else out_specs,
        scratch_shapes=list(scratch),
        compiler_params=PARAMS,
        cost_estimate=pl.CostEstimate(
            flops=us * 1_000_000, bytes_accessed=us * 3_000_000, transcendentals=0
        ),
        name=name,
    )(*args)


def solution(mesh):
    route = routes(mesh)
    vmem = lambda *shape: pltpu.VMEM(shape, jnp.float32)
    inside = pl.BlockSpec(memory_space=pltpu.VMEM)
    outside = pl.BlockSpec(memory_space=pltpu.HBM)
    unread = pl.BlockSpec(memory_space=pl.ANY)
    far = lambda x: pltpu.with_memory_space_constraint(x, pltpu.HBM)

    def sent(x, pairs):
        return lax.ppermute(x, AXES, pairs)

    def per_device(adjoint, source, jacobian, couple, donor_row, target_row, tile_count, weights):
        nv, na, nr, nc = adjoint.shape[1:]
        donors, slots = donor_row.shape[2:]
        count = len(route["faces"])
        sides = 2 * nv * na
        edges = lambda across: [vmem(sides + SUB, nc), vmem(sides, nc), vmem(across, nc), vmem(nr, nc)]
        block = vmem(nv, na, nr, nc)
        edge_forms = lambda n: [vmem(n, nv, nr, nc)] + [vmem(n, nv, 2 * na, nc)] * 2
        lam, cpl, rhs, *tiles = call(
            load_kernel, "load",
            [block, vmem(12, na, nr, nc), block] + [vmem(4 * slots * nv + SUB * (count - 1 - n), nc) for n in range(count)],
            [*map(far, (adjoint[0], donor_row[0], couple[0], source[0]))], [outside] * 4,
            [pltpu.SMEM(donor_row.shape[1:], jnp.int32), pltpu.SemaphoreType.DMA((4,))],
        )
        ahead, back, cross, cols = call(pack_kernel, "pack", edges(sides - SUB), [lam])
        tiles = [sent(x, pairs) for x, pairs in zip(tiles, route["faces"])]
        for sweep in range(SWEEPS):
            last = sweep == SWEEPS - 1
            ahead = sent(ahead, route["ahead"])
            back = sent(back, route["back"])
            across = sent(cross, route["across"])
            if sweep == 0:
                share = shares(count)
                jac, placed, inv, edge_coefs, row_coefs, *matrices = call(
                    fetch_kernel, "fetch",
                    [vmem(nv, nv, na, nr, nc), vmem(donors, slots, nr, nc), vmem(na, nr, nc),
                     vmem(2, nr, nc), vmem(4, 2 * na, nc), *edge_forms(nv // 2)],
                    [cpl, *map(far, (jacobian[0], target_row[0], tile_count[0], weights.reshape(-1, nc)))],
                    [inside] + [outside] * 4,
                    [pltpu.SMEM(target_row.shape[1:], jnp.int32), pltpu.SMEM(tile_count.shape[1:], jnp.int32),
                     pltpu.VMEM((donors * slots, nc), jnp.float32), pltpu.SemaphoreType.DMA((nv + 3,))],
                )
                relayed = [
                    call(functools.partial(relay_kernel, share * n, share=share), f"relay{n}",
                         [vmem(share + 2 * slots * nv, nc)], [cols, x, inv], [inside] * 2 + [unread])[0]
                    for n, x in enumerate(tiles)
                ]
                relayed = [sent(x, route["mate"]) for x in relayed]
                base, rhs, *more = call(
                    functools.partial(local_kernel, True), "local0", [block] * 2 + edge_forms(nv - nv // 2), [lam, cpl, jac, rhs, inv, placed, *tiles]
                )
                matrices += more
                lam, rhs, ahead, back, cross, cols = call(
                    functools.partial(finish_kernel, count, False), "finish0", [block] * 2 + edges(nr),
                    [base, edge_coefs, row_coefs, *matrices, ahead, back, across, rhs, inv, placed, *relayed],
                )
                continue
            mate = sent(cols, route["mate"])
            base = call(
                functools.partial(local_kernel, False), f"local{sweep}", [block], [lam, cpl, jac, rhs, inv]
            )[0]
            scratch, spaces, outs = [], None, [block] + edges(nr)
            if last:
                outs, spaces = [jax.ShapeDtypeStruct((nv, na, nr, nc), jnp.float32)], [outside]
                scratch = [pltpu.VMEM((nv, na, nr, nc), jnp.float32), pltpu.SemaphoreType.DMA((nv,))]
            lam, *more = call(
                functools.partial(finish_kernel, 0, last), f"finish{sweep}", outs,
                [base, edge_coefs, row_coefs, *matrices, ahead, back, across, mate], None, scratch, 1, spaces,
            )
            if not last:
                ahead, back, cross, cols = more
        return lam[None]

    in_specs = (
        P("sec", None, None, "rad", "circ"),
        P("sec", None, None, "rad", "circ"),
        P("sec", None, None, None, "rad", "circ"),
        P("sec", None, None, "rad", "circ"),
        P("rad", None, None, None),
        P("rad", None, None, None),
        P("rad", None, None),
        P("rad", None, "circ", None, None),
    )
    out_specs = P("sec", None, None, "rad", "circ")
    return jax.shard_map(
        per_device, mesh=mesh, in_specs=in_specs, out_specs=out_specs, check_vma=False
    )
```
